256 devices in a mesh: dom: 256 (over x, y, z, core).
Axes of the slice: x: 4, y: 4, z: 8, core: 2. Of those that a mesh axis runs over, the one named last changes fastest.
Arguments:
- x_block: float32 [8, 393216], P(None, 'dom'), may hold values from -18 to 18
- p_block: float32 [8, 393216], P(None, 'dom'), may hold values from -18 to 18
- stiff_elem: float32 [20, 20, 65536], P(None, None, 'dom'), may hold values from -6 to 12.4, as said below
- mass_elem: float32 [20, 20, 65536], P(None, None, 'dom'), may hold values from -0.03 to 0.7, as said below
- node_elem: float32 [10, 10, 65536], P(None, None, 'dom'), may hold values from -1 to 6.1, as said below
- elem_edge: int32 [20, 65536], P(None, 'dom'), may hold values from 0 to 1919, as said below
- elem_node: int32 [10, 65536], P(None, 'dom'), may hold values from 0 to 575, as said below
- send_edge: int32 [6, 16384], P(None, 'dom'), may hold values from 0 to 1535, as said below
- send_node: int32 [6, 8192], P(None, 'dom'), may hold values from 0 to 383, as said below
- grad_pairs: int32 [2, 393216], P(None, 'dom'), may hold values from 0 to 575, as said below
Outputs:
- w_block: float32 [8, 393216], P(None, 'dom')
- gram_stiff: float32 [24, 24], replicated
- gram_mass: float32 [24, 24], replicated
The draws below stay inside these ranges and needn't reach their ends.
Inputs may be any that keep to these rules, and one draw needn't show every extreme that they name: `stiff_elem`: each element's matrix is symmetric and positive definite. `mass_elem`: each element's matrix is symmetric and positive definite. `node_elem`: each element's matrix is symmetric and positive definite. `elem_edge`: the 20 entries of one element are distinct, and every entry of a subdomain's extended edge list is used by some element of that subdomain. `elem_node`: the 10 entries of one element are distinct, and every entry of a subdomain's extended nodal list is used by some element of that subdomain. `send_edge`: the 64 entries of one direction of one subdomain are distinct. `send_node`: the 32 entries of one direction of one subdomain are distinct. `grad_pairs`: the tail and head of one edge unknown differ.
All inputs are finite; a program needn't handle non-finite values.
Results may differ from the reference program's by a relative error of at most 0.0001.
Values sent between devices are 32-bit elements; how exact they have to be, the bound alone decides.
A program may use at most 128 MiB of HBM per device.

```python
import math
import jax
import jax.numpy as jnp
import numpy as np
from jax import lax

EL = 256
MODES = 8
EDOF = 20
NDOF = 10
CHEB_DEG = 3
DOMAINS = 256
NEDGE = 1536
NNODE = 384
GE = 64
GN = 32
TOTAL_EL = 65536
TOTAL_EDGE = 393216
TOTAL_NODE = 98304


def device_scale(devices, per_device):
    position = (jnp.arange(devices * per_device) // per_device).astype(jnp.float32)
    return 1.0 + 2.0 * position / max(devices - 1, 1)


def block_draw(key, salt):
    devices = TOTAL_EDGE // NEDGE
    subkeys = jax.random.split(jax.random.fold_in(key, salt), 1)
    values = jnp.clip(jax.random.normal(subkeys[0], (MODES, TOTAL_EDGE), jnp.float32), -5.0, 5.0)
    return values * device_scale(devices, NEDGE)[None, :]


def local_tables():
    tetra_edges = [(0, 1), (0, 2), (0, 3), (1, 2), (1, 3), (2, 3)]
    middle = {}
    for number, couple in enumerate(tetra_edges):
        middle[couple] = 4 + number
    edge_links = []
    for couple in tetra_edges:
        edge_links.append((couple[0], middle[couple]))
        edge_links.append((middle[couple], couple[1]))
    faces = [(0, 1, 2), (0, 1, 3), (0, 2, 3), (1, 2, 3)]
    cycles = []
    for corner_one, corner_two, corner_three in faces:
        front_middle = middle[corner_one, corner_two]
        side_middle = middle[corner_one, corner_three]
        back_middle = middle[corner_two, corner_three]
        edge_links.append((front_middle, side_middle))
        edge_links.append((front_middle, back_middle))
        cycles.append([corner_one, front_middle, side_middle])
        cycles.append([corner_two, back_middle, front_middle])
        cycles.append([corner_three, side_middle, front_middle, back_middle])
    node_rows = np.zeros((len(edge_links), 10), np.float32)
    for row_number, couple in enumerate(edge_links):
        node_rows[row_number, couple[0]] = -1.0
        node_rows[row_number, couple[1]] = 1.0
    curl_rows = np.zeros((len(cycles), 20), np.float32)
    for row_number, cycle_nodes in enumerate(cycles):
        for position in range(len(cycle_nodes)):
            anchor = cycle_nodes[position]
            target = cycle_nodes[(position + 1) % len(cycle_nodes)]
            for number, couple in enumerate(edge_links):
                if couple == (anchor, target):
                    curl_rows[row_number, number] += 1.0
                if couple == (target, anchor):
                    curl_rows[row_number, number] -= 1.0
    return (curl_rows, node_rows)


def operator_draw(key, salt, rows, size, norm, ramped):
    count = rows.shape[0]
    subkeys = jax.random.split(jax.random.fold_in(key, salt), 3)
    weights = jnp.exp(jax.random.uniform(subkeys[0], (count, TOTAL_EL), jnp.float32, 0.0, math.log(10.0)))
    scale = jnp.exp(jax.random.uniform(subkeys[2], (TOTAL_EL,), jnp.float32, 0.0, math.log(10.0)))
    matrix = jnp.zeros((size, size, TOTAL_EL), jnp.float32)
    for row_number in range(count):
        outer_table = np.outer(rows[row_number], rows[row_number]).astype(np.float32)
        matrix = matrix + jnp.asarray(outer_table)[:, :, None] * weights[row_number][None, None, :]
    unit = jnp.eye(size, dtype=jnp.float32)[:, :, None]
    lift = jax.random.uniform(subkeys[1], (size, 1, TOTAL_EL), jnp.float32, 0.3, 0.6)
    matrix = matrix + unit * lift
    if ramped:
        scale = scale * device_scale(TOTAL_EL // EL, EL)
    return matrix * (scale / norm)[None, None, :]


def definite_draw(key, salt, size, lower, upper, ramped):
    subkeys = jax.random.split(jax.random.fold_in(key, salt), 3)
    raw = jax.random.uniform(subkeys[0], (size, size, TOTAL_EL), jnp.float32, -1.0, 1.0)
    scale = jnp.exp(jax.random.uniform(subkeys[2], (TOTAL_EL,), jnp.float32, math.log(lower), math.log(upper)))
    mirror = 0.5 * (raw + jnp.swapaxes(raw, 0, 1))
    unit = jnp.eye(size, dtype=jnp.float32)[:, :, None]
    lift = jax.random.uniform(subkeys[1], (size, 1, TOTAL_EL), jnp.float32, 1.1, 1.4)
    matrix = mirror * (1.0 - unit) + unit * lift * (size - 1)
    if ramped:
        scale = scale * device_scale(TOTAL_EL // EL, EL)
    return matrix * (scale / (8.0 * size))[None, None, :]


def shuffled_lists(key, salt, count, length):
    subkeys = jax.random.split(jax.random.fold_in(key, salt), count)

    def shuffle_single(single):
        return jax.random.permutation(single, length)
    return jax.vmap(shuffle_single)(subkeys)


def connect_draw(key, salt, width, length):
    devices = TOTAL_EL // EL
    shuffled = shuffled_lists(key, salt, devices, length)
    picks = shuffled[:, jnp.arange(EL * width) % length]
    return picks.reshape(devices, EL, width).transpose(2, 0, 1).reshape(width, TOTAL_EL).astype(jnp.int32)


def fresh_connect_draw(key, salt, width, length):
    devices = TOTAL_EL // EL
    rounds = (EL * width + length - 1) // length
    shuffled = shuffled_lists(key, salt, devices * rounds, length).reshape(devices, rounds * length)
    picks = shuffled[:, :EL * width]
    return picks.reshape(devices, EL, width).transpose(2, 0, 1).reshape(width, TOTAL_EL).astype(jnp.int32)


def sends_draw(key, salt, owned, ghosts):
    devices = TOTAL_EL // EL
    shuffled = shuffled_lists(key, salt, 6 * devices, owned)
    return shuffled[:, :ghosts].reshape(6, devices * ghosts).astype(jnp.int32)


def draw_x_block(key, part):
    return block_draw(key, 11)


def draw_p_block(key, part):
    return block_draw(key, 12)


def draw_stiff_elem(key, part):
    curl_rows, node_rows = local_tables()
    return operator_draw(key, 13, curl_rows, EDOF, 50.0, True)


def draw_mass_elem(key, part):
    return definite_draw(key, 14, EDOF, 1.0, 4.0, False)


def draw_node_elem(key, part):
    curl_rows, node_rows = local_tables()
    return operator_draw(key, 15, node_rows, NDOF, 100.0, False)


def draw_elem_edge(key, part):
    return fresh_connect_draw(key, 21, EDOF, NEDGE + 6 * GE)


def draw_elem_node(key, part):
    return connect_draw(key, 22, NDOF, NNODE + 6 * GN)


def draw_send_edge(key, part):
    return sends_draw(key, 23, NEDGE, GE)


def draw_send_node(key, part):
    return sends_draw(key, 24, NNODE, GN)


def draw_grad_pairs(key, part):
    devices = TOTAL_EL // EL
    length = NNODE + 6 * GN
    shuffled = shuffled_lists(key, 25, devices, length)
    offsets = jax.random.randint(jax.random.fold_in(key, 26), (devices, 1), 1, length)
    position = jnp.arange(NEDGE) % length
    tails = shuffled[:, position]
    heads = jnp.take_along_axis(shuffled, (position[None, :] + offsets) % length, axis=1)
    return jnp.stack([tails.reshape(-1), heads.reshape(-1)]).astype(jnp.int32)


def setup_inputs(seed: int = 0) -> dict:
    key_of = jax.random.split(jax.random.key(seed), 11)
    x_block = draw_x_block(jax.random.fold_in(key_of[10], 71), 0)
    p_block = draw_p_block(jax.random.fold_in(key_of[10], 71), 0)
    stiff_elem = draw_stiff_elem(jax.random.fold_in(key_of[10], 71), 0)
    mass_elem = draw_mass_elem(jax.random.fold_in(key_of[10], 71), 0)
    node_elem = draw_node_elem(jax.random.fold_in(key_of[10], 71), 0)
    elem_edge = draw_elem_edge(jax.random.fold_in(key_of[10], 71), 0)
    elem_node = draw_elem_node(jax.random.fold_in(key_of[10], 71), 0)
    send_edge = draw_send_edge(jax.random.fold_in(key_of[10], 71), 0)
    send_node = draw_send_node(jax.random.fold_in(key_of[10], 71), 0)
    grad_pairs = draw_grad_pairs(jax.random.fold_in(key_of[10], 71), 0)
    return {"x_block": x_block, "p_block": p_block, "stiff_elem": stiff_elem, "mass_elem": mass_elem, "node_elem": node_elem, "elem_edge": elem_edge, "elem_node": elem_node, "send_edge": send_edge, "send_node": send_node, "grad_pairs": grad_pairs}


highest = lax.Precision.HIGHEST
OFFSETS = (1, -1, 4, -4, 16, -16)
interval_low = 0.3
interval_high = 1.7
jacobi_weight = 0.7


def ghost_map(send_list, owned, ghosts):
    device_ids = jnp.arange(DOMAINS, dtype=jnp.int32)
    pieces = [device_ids[:, None] * owned + jnp.arange(owned, dtype=jnp.int32)[None, :]]
    shared = send_list.reshape(6, DOMAINS, ghosts)
    for direction in range(6):
        source = (device_ids - OFFSETS[direction]) % DOMAINS
        pieces.append(source[:, None] * owned + shared[direction][source])
    return jnp.concatenate(pieces, axis=1).astype(jnp.int32)


def element_apply(matrices, connect, mapping, vectors):
    def one_device(index, total):
        start = (index * EL).astype(jnp.int32)
        matrix = lax.dynamic_slice_in_dim(matrices, start, EL, 2)
        links = lax.dynamic_slice_in_dim(connect, start, EL, 1)
        columns = mapping[index][links]
        values = vectors[:, columns]
        terms = jnp.einsum("jke,cke->cje", matrix, values, precision=highest)
        return total.at[:, columns].add(terms)

    return lax.fori_loop(0, DOMAINS, one_device, jnp.zeros_like(vectors))


def assemble_diag(matrices, connect, mapping, length):
    def one_device(index, total):
        start = (index * EL).astype(jnp.int32)
        matrix = lax.dynamic_slice_in_dim(matrices, start, EL, 2)
        links = lax.dynamic_slice_in_dim(connect, start, EL, 1)
        columns = mapping[index][links]
        diagonal = jnp.einsum("jje->je", matrix)
        return total.at[columns].add(diagonal)

    return lax.fori_loop(0, DOMAINS, one_device, jnp.zeros((length,), jnp.float32))


def reference(x_block, p_block, stiff_elem, mass_elem, node_elem, elem_edge, elem_node, send_edge, send_node, grad_pairs):
    edge_map = ghost_map(send_edge, NEDGE, GE)
    node_map = ghost_map(send_node, NNODE, GN)
    stiff_x = element_apply(stiff_elem, elem_edge, edge_map, x_block)
    mass_x = element_apply(mass_elem, elem_edge, edge_map, x_block)
    quotient = jnp.sum(x_block * stiff_x, axis=1) / jnp.sum(x_block * mass_x, axis=1)
    residual = stiff_x - quotient[:, None] * mass_x
    edge_diag = assemble_diag(stiff_elem, elem_edge, edge_map, TOTAL_EDGE)
    node_diag = assemble_diag(node_elem, elem_node, node_map, TOTAL_NODE)
    center = 0.5 * (interval_high + interval_low)
    spread = 0.5 * (interval_high - interval_low)
    sigma = center / spread
    rho_now = 1.0 / sigma
    step_dir = residual / (center * edge_diag)
    smooth = step_dir
    for turn in range(CHEB_DEG - 1):
        rho_next = 1.0 / (2.0 * sigma - rho_now)
        remain = residual - element_apply(stiff_elem, elem_edge, edge_map, smooth)
        step_dir = rho_next * rho_now * step_dir + (2.0 * rho_next / spread) * remain / edge_diag
        smooth = smooth + step_dir
        rho_now = rho_next
    after = residual - element_apply(stiff_elem, elem_edge, edge_map, smooth)
    edge_owner = jnp.arange(TOTAL_EDGE, dtype=jnp.int32) // NEDGE
    tails = node_map[edge_owner, grad_pairs[0]]
    heads = node_map[edge_owner, grad_pairs[1]]
    nodal_res = jnp.zeros((MODES, TOTAL_NODE), jnp.float32).at[:, heads].add(after).at[:, tails].add(-after)
    first = jacobi_weight * nodal_res / node_diag
    second = first + jacobi_weight * (nodal_res - element_apply(node_elem, elem_node, node_map, first)) / node_diag
    w_block = smooth + second[:, heads] - second[:, tails]
    basis = jnp.concatenate([x_block, w_block, p_block], axis=0)
    stiff_basis = element_apply(stiff_elem, elem_edge, edge_map, basis)
    mass_basis = element_apply(mass_elem, elem_edge, edge_map, basis)
    gram_stiff = jnp.einsum("cn,dn->cd", basis, stiff_basis, precision=highest) / TOTAL_EDGE
    gram_mass = jnp.einsum("cn,dn->cd", basis, mass_basis, precision=highest) / TOTAL_EDGE
    return w_block, gram_stiff, gram_mass
```

```python
import jax
import jax.numpy as jnp
from jax import lax
from jax.experimental import pallas as pl
from jax.experimental.pallas import tpu as pltpu
from jax.sharding import PartitionSpec as P

CHEB_DEG = 3
OFFSETS = (1, 4, 16)
LOW = 16
LANES = 128
EDOF = 20
NDOF = 10
EB = 12
EG = 15
NB = 3
NG = 5
ECOL = EDOF * 256
NCOL = NDOF * 256
GCOL = 2 * 1536
interval_low = 0.3
interval_high = 1.7
jacobi_weight = 0.7

f32 = jnp.float32
bf16 = jnp.bfloat16
MESH = pl.DeviceIdType.MESH

X_PAIR, X_DIAG, X_IMAGE, X_FIRST, X_NDIAG, X_CHEB = 0, 1, 2, 3, 4, 5
X_NODE = X_CHEB + 5
X_W = X_NODE + 4
COUNTS = (2, 1, 2, 2, 1) + (1,) * 10


def take(values, lanes):
    return jnp.take_along_axis(values, lanes, axis=1)


def split(values):
    high = values.astype(bf16).astype(f32)
    return jnp.concatenate([high, values - high], axis=0).astype(bf16)


def spread_row(row):
    return jnp.broadcast_to(row, (8, row.shape[1]))


def cols(start, size=LANES):
    return pl.ds(pl.multiple_of(start, LANES), size)


def kernel(
    devices,
    x_ref,
    p_ref,
    stiff_ref,
    mass_ref,
    nodal_ref,
    elem_edge_ref,
    elem_node_ref,
    send_edge_ref,
    send_node_ref,
    grad_ref,
    w_ref,
    gram_s_ref,
    gram_m_ref,
    xe,
    pe,
    ve,
    ne,
    vx,
    vp,
    vv,
    nv,
    gv,
    er,
    ec,
    nr,
    nc,
    gr,
    gc,
    sr,
    sc,
    tr,
    tc,
    inv_e,
    inv_n,
    oh_e,
    qm_e,
    oh_n,
    qm_n,
    oh_g,
    qm_g,
    st,
    left,
    basis_t,
    image_t,
    tot,
    tot2,
    res,
    recip,
    step,
    nres,
    nrecip,
    nfirst,
    ntot,
    send_bufs,
    recv_bufs,
    ar_send,
    ar_recv,
    send_sems,
    recv_sems,
    ar_send_sems,
    ar_recv_sems,
):
    me = lax.axis_index("dom")
    low, high = lax.rem(me, LOW), lax.div(me, LOW)
    highs = devices // LOW
    around = []
    for offset in OFFSETS:
        around.append(lax.rem(me + offset, devices))
        around.append(lax.rem(me + devices - offset, devices))
    groups = [
        [high * LOW + lax.rem(low + m, LOW) for m in range(1, LOW)],
        [lax.rem(high + m, highs) * LOW + low for m in range(1, highs)],
    ]

    barrier = pltpu.get_barrier_semaphore()
    everyone = around + groups[0] + groups[1]
    for partner in everyone:
        pl.semaphore_signal(barrier, inc=1, device_id=(partner,), device_id_type=MESH)

    lane8 = lax.broadcasted_iota(jnp.int32, (8, LANES), 1)
    row8 = lax.broadcasted_iota(jnp.int32, (8, LANES), 0)
    lane128 = lax.broadcasted_iota(jnp.int32, (LANES, LANES), 1).astype(f32)
    zero8 = jnp.zeros((8, LANES), f32)

    def launch(e, t):
        for side in range(2):
            pltpu.make_async_remote_copy(
                src_ref=send_bufs[e].at[t],
                dst_ref=recv_bufs[e].at[2 * t + side],
                send_sem=send_sems.at[e],
                recv_sem=recv_sems.at[e],
                device_id=(around[2 * t + side],),
                device_id_type=MESH,
            ).start()

    def whole(e):
        return pltpu.make_async_remote_copy(
            src_ref=recv_bufs[e],
            dst_ref=recv_bufs[e],
            send_sem=send_sems.at[e],
            recv_sem=recv_sems.at[e],
            device_id=(around[0],),
            device_id_type=MESH,
        )

    def arrived(e):
        whole(e).wait_recv()

    def edge_tile(e, i, t, back):
        first, second = (2 * t + 1, 2 * t) if back else (2 * t, 2 * t + 1)
        return jnp.where(lane8 < 64, recv_bufs[e][first, i], recv_bufs[e][second, i])

    def node_tile(e, n, back):
        swap = 1 if back else 0
        if n == 1:
            tile = jnp.where(lane8 < 32, recv_bufs[e][4 ^ swap, 0], recv_bufs[e][5 ^ swap, 0])
            return jnp.where(lane8 < 64, tile, 0.0)
        one = jnp.where(lane8 < 32, recv_bufs[e][0 ^ swap, 0], recv_bufs[e][1 ^ swap, 0])
        two = jnp.where(lane8 < 96, recv_bufs[e][2 ^ swap, 0], recv_bufs[e][3 ^ swap, 0])
        return jnp.where(lane8 < 64, one, two)

    def reduce_start(slot, stage, tile):
        mine = (low, high)[stage]
        ar_send[slot] = tile
        ar_recv[slot, mine] = tile
        for partner in groups[stage]:
            pltpu.make_async_remote_copy(
                src_ref=ar_send.at[slot],
                dst_ref=ar_recv.at[slot, mine],
                send_sem=ar_send_sems.at[slot],
                recv_sem=ar_recv_sems.at[slot],
                device_id=(partner,),
                device_id_type=MESH,
            ).start()

    def reduce_whole(slot, stage):
        part = ar_recv.at[slot, pl.ds(0, (LOW, highs)[stage] - 1)]
        return pltpu.make_async_remote_copy(
            src_ref=part,
            dst_ref=part,
            send_sem=ar_send_sems.at[slot],
            recv_sem=ar_recv_sems.at[slot],
            device_id=(around[0],),
            device_id_type=MESH,
        )

    def reduce_finish(slot, stage):
        reduce_whole(slot, stage).wait_recv()
        parts = [ar_recv[slot, i] for i in range((LOW, highs)[stage])]
        while len(parts) > 1:
            parts = [a + b for a, b in zip(parts[::2], parts[1::2])]
        return parts[0]

    def gather(out, lanes, blocks, count, sources, first, last, unroll):
        def body(i, carry):
            r, c = lanes[i], blocks[i]
            for o, s in zip(out, sources):
                value = zero8 if first == 0 else o[i]
                for k in range(first, last):
                    value = jnp.where(c == k, take(s[k], r), value)
                o[i] = value
            return carry

        lax.fori_loop(0, count, body, 0, unroll=unroll)

    def pick(source, lanes, blocks, t, owned):
        value = zero8
        for k in range(owned):
            value = jnp.where(blocks[t] == k, take(source[k], lanes[t]), value)
        return value

    def returned(inverse, tiles, block, per):
        value = None
        for d in range(6):
            where = inverse[block * 6 + d]
            term = jnp.where(where >= LANES, take(tiles[d // per], where & 127), 0.0)
            value = term if value is None else value + term
        return value

    def index_tables(row, lanes, blocks, i):
        lanes[i] = spread_row(row & 127)
        blocks[i] = spread_row(row >> 7)

    def masks(qm, blocks, count, parts):
        def body(i, carry):
            c = blocks[i]
            for q in range(parts):
                one = jnp.where(c == q, 1.0, 0.0)
                qm[pl.ds(16 * q, 16), cols(i * LANES)] = jnp.concatenate([one, one], 0).astype(bf16)
            return carry

        lax.fori_loop(0, count, body, 0, unroll=2)

    def one_hot(column):
        return jnp.where(jnp.broadcast_to(column, (LANES, LANES)) == lane128, 1.0, 0.0).astype(bf16)

    def columns_of(rows):
        count, width = rows.shape
        padded = -count % 8
        if padded:
            rows = jnp.concatenate([rows, jnp.zeros((padded, width), jnp.int32)], axis=0)
        return (rows & 127).astype(f32).T

    def fill(base, qm, first, last, count, source, unroll=2):
        def body(i, carry):
            term = st[pl.ds(source, 16), cols(i * LANES)]
            for q in range(first, last):
                left[pl.ds(base + 16 * (q - first), 16), cols(i * LANES)] = (
                    term * qm[pl.ds(16 * q, 16), cols(i * LANES)]
                )
            return carry

        lax.fori_loop(0, count, body, 0, unroll=unroll)

    def scatter(rows, width, table):
        return jnp.dot(left[0:rows, 0:width], table[...], preferred_element_type=f32)

    def joined(product, q):
        return product[16 * q : 16 * q + 8] + product[16 * q + 8 : 16 * q + 16]

    def apply(matrix, values, size, group, consume):
        def body(jj, carry):
            for h in range(2):
                total = [None] * group
                for k in range(size):
                    value = values[2 * k + h]
                    for u in range(group):
                        row = matrix[jj * group + u, pl.ds(k, 1), pl.ds(LANES * h, LANES)]
                        term = row * value
                        total[u] = term if k == 0 else total[u] + term
                for u in range(group):
                    carry = consume(2 * (jj * group + u) + h, total[u], carry)
            return carry

        return body

    def shared_rows(ref, width, per, tiles):
        rows = []
        for t in range(tiles):
            pieces = [ref[d : d + 1, :] for d in range(t * per, min(6, (t + 1) * per))]
            missing = per - len(pieces)
            if missing:
                pieces.append(jnp.zeros((1, missing * width), jnp.int32))
            rows.append(jnp.concatenate(pieces, axis=1))
        return rows

    edge_rows = shared_rows(send_edge_ref, 64, 2, 3)
    for t in range(3):
        index_tables(edge_rows[t], sr, sc, t)
    for k in range(EB):
        xe[k] = x_ref[:, LANES * k : LANES * (k + 1)]
        pe[k] = p_ref[:, LANES * k : LANES * (k + 1)]
    for t in range(3):
        send_bufs[X_PAIR][t, 0] = pick(xe, sr, sc, t, EB)
        send_bufs[X_PAIR][t, 1] = pick(pe, sr, sc, t, EB)
    pl.semaphore_wait(barrier, len(everyone))
    for t in range(3):
        launch(X_PAIR, t)

    for j in range(EDOF):
        for h in range(2):
            row = elem_edge_ref[j : j + 1, LANES * h : LANES * (h + 1)]
            index_tables(row, er, ec, 2 * j + h)
    edge_columns = columns_of(elem_edge_ref[...])
    for j in range(EDOF):
        for h in range(2):
            oh_e[256 * j + LANES * h : 256 * j + LANES * (h + 1), :] = one_hot(
                edge_columns[LANES * h : LANES * (h + 1), j : j + 1]
            )
    masks(qm_e, ec, 2 * EDOF, EG)

    for j in range(EDOF):
        for h in range(2):
            diagonal = spread_row(stiff_ref[j, j : j + 1, LANES * h : LANES * (h + 1)])
            st[0:16, 256 * j + LANES * h : 256 * j + LANES * (h + 1)] = split(diagonal)
    fill(0, qm_e, 0, EG, 2 * EDOF, 0)
    product = scatter(16 * EG, ECOL, oh_e)
    for t in range(3):
        send_bufs[X_DIAG][t, 0] = joined(product, EB + t)
        launch(X_DIAG, t)
    for k in range(EB):
        recip[k] = joined(product, k)

    gather([vx], er, ec, 2 * EDOF, [xe], 0, EB, 4)

    def inverse_lists(inverse, rows, lanes, blocks, per, owned):
        tiles = len(rows)
        width = LANES * tiles
        shared = jnp.concatenate(rows, axis=0)
        turned = columns_of(shared)
        table = jnp.concatenate([one_hot(turned[:, t : t + 1]) for t in range(tiles)], axis=0)
        parts = []
        for q in range(0, owned + owned % 2):
            line = []
            for t in range(tiles):
                direction = t * per + lane8 // (LANES // per)
                keep = jnp.logical_and(row8 == direction, blocks[t] == q)
                line.append(jnp.where(keep, LANES + lane8, 0).astype(f32))
            parts.append(jnp.concatenate(line, axis=1))
        found = jnp.dot(
            jnp.concatenate(parts, axis=0).astype(bf16), table, preferred_element_type=f32
        ).astype(jnp.int32)
        for q in range(owned):
            for d in range(6):
                inverse[q * 6 + d] = spread_row(found[8 * q + d : 8 * q + d + 1])

    inverse_lists(inv_e, edge_rows, sr, sc, 2, EB)

    arrived(X_PAIR)
    for t in range(3):
        xe[EB + t] = edge_tile(X_PAIR, 0, t, False)
        pe[EB + t] = edge_tile(X_PAIR, 1, t, False)
    gather([vx], er, ec, 2 * EDOF, [xe], EB, EG, 4)

    def keep_terms(base, store, ghost_base, i, total):
        term = split(total)
        place = cols(i * LANES)
        if store is not None:
            image_t[pl.ds(store, 16), place] = term
        if base is not None:
            st[pl.ds(base, 16), place] = term
            for q in range(EB, EG):
                left[pl.ds(ghost_base + 16 * (q - EB), 16), place] = term * qm_e[pl.ds(16 * q, 16), place]

    def x_consume(base, store, ghost_base):
        def consume(i, total, carry):
            keep_terms(base, store, ghost_base, i, total)
            return carry + total * vx[i]

        return consume

    numerator = lax.fori_loop(0, 5, apply(stiff_ref, vx, EDOF, 4, x_consume(0, 0, 0)), zero8)
    denominator = lax.fori_loop(0, 5, apply(mass_ref, vx, EDOF, 4, x_consume(16, 16, 48)), zero8)
    product = scatter(96, ECOL, oh_e)
    for t in range(3):
        send_bufs[X_IMAGE][t, 0] = joined(product, t)
        send_bufs[X_IMAGE][t, 1] = joined(product, 3 + t)
        launch(X_IMAGE, t)
    numerator = jnp.sum(numerator, axis=1, keepdims=True)
    denominator = jnp.sum(denominator, axis=1, keepdims=True)
    reduce_start(0, 0, jnp.where(lane8 == 0, numerator, jnp.where(lane8 == 1, denominator, 0.0)))
    fill(0, qm_e, 0, EB, 2 * EDOF, 0)
    fill(16 * EB, qm_e, 0, EB, 2 * EDOF, 16)
    product = scatter(32 * EB, ECOL, oh_e)
    for k in range(EB):
        tot[k] = joined(product, k)
        tot2[k] = joined(product, EB + k)
    arrived(X_DIAG)
    tiles = [edge_tile(X_DIAG, 0, t, True) for t in range(3)]
    center = 0.5 * (interval_high + interval_low)
    spread = 0.5 * (interval_high - interval_low)
    for k in range(EB):
        recip[k] = 1.0 / (recip[k] + returned(inv_e, tiles, k, 2))
    reduce_start(1, 1, reduce_finish(0, 0))
    arrived(X_IMAGE)
    for i, total in enumerate((tot, tot2)):
        tiles = [edge_tile(X_IMAGE, i, t, True) for t in range(3)]
        for k in range(EB):
            total[k] = total[k] + returned(inv_e, tiles, k, 2)
            pe_scaled = total[k] * recip[k] * (1.0 / center)
            (ve if i == 0 else step)[k] = pe_scaled
    for t in range(3):
        send_bufs[X_FIRST][t, 0] = pick(ve, sr, sc, t, EB)
        send_bufs[X_FIRST][t, 1] = pick(step, sr, sc, t, EB)
        launch(X_FIRST, t)

    node_rows = shared_rows(send_node_ref, 32, 4, 2)
    for t in range(2):
        index_tables(node_rows[t], tr, tc, t)
    for j in range(NDOF):
        for h in range(2):
            row = elem_node_ref[j : j + 1, LANES * h : LANES * (h + 1)]
            index_tables(row, nr, nc, 2 * j + h)
    node_columns = columns_of(elem_node_ref[...])
    for j in range(NDOF):
        for h in range(2):
            oh_n[256 * j + LANES * h : 256 * j + LANES * (h + 1), :] = one_hot(
                node_columns[LANES * h : LANES * (h + 1), j : j + 1]
            )
    masks(qm_n, nc, 2 * NDOF, NG)

    sums = reduce_finish(1, 1)
    quotient = jnp.broadcast_to(sums[:, 0:1] / sums[:, 1:2], (8, LANES))
    for k in range(EB):
        residual = tot[k] - quotient * tot2[k]
        res[k] = residual
        first_step = residual * recip[k] * (1.0 / center)
        step[k] = first_step
        ve[k] = first_step

    def stiff_image(extend, back):
        gather([vv], er, ec, 2 * EDOF, [ve], 0, EB, 4)
        arrived(extend)
        for t in range(3):
            tile = edge_tile(extend, 0, t, False)
            if extend == X_FIRST:
                tile = tile - quotient * edge_tile(extend, 1, t, False)
            ve[EB + t] = tile
        gather([vv], er, ec, 2 * EDOF, [ve], EB, EG, 4)

        def consume(i, total, carry):
            keep_terms(0, None, 0, i, total)
            return carry

        lax.fori_loop(0, 5, apply(stiff_ref, vv, EDOF, 4, consume), 0)
        product = scatter(48, ECOL, oh_e)
        for t in range(3):
            send_bufs[back][t, 0] = joined(product, t)
            launch(back, t)
        fill(0, qm_e, 0, EB, 2 * EDOF, 0)
        product = scatter(16 * EB, ECOL, oh_e)
        for k in range(EB):
            tot[k] = joined(product, k)
        return back

    def image_block(tiles, k):
        return tot[k] + returned(inv_e, tiles, k, 2)

    sigma = center / spread
    rho_now = 1.0 / sigma
    extend = X_FIRST
    for turn in range(CHEB_DEG - 1):
        rho_next = 1.0 / (2.0 * sigma - rho_now)
        back = X_CHEB + 2 * turn
        stiff_image(extend, back)
        if turn == 0:
            for j in range(NDOF):
                for h in range(2):
                    diagonal = spread_row(nodal_ref[j, j : j + 1, LANES * h : LANES * (h + 1)])
                    st[0:16, 256 * j + LANES * h : 256 * j + LANES * (h + 1)] = split(diagonal)
            fill(0, qm_n, 0, NG, 2 * NDOF, 0)
            product = scatter(16 * NG, NCOL, oh_n)
            for t in range(3):
                send_bufs[X_NDIAG][t, 0] = joined(product, NB + t // 2)
                launch(X_NDIAG, t)
            for k in range(NB):
                nrecip[k] = joined(product, k)
            inverse_lists(inv_n, node_rows, tr, tc, 4, NB)
        else:
            for side in range(2):
                for k in range(EB):
                    row = grad_ref[1 - side : 2 - side, LANES * k : LANES * (k + 1)]
                    index_tables(row, gr, gc, side * EB + k)
            grad_columns = columns_of(grad_ref[...])
            for side in range(2):
                for k in range(EB):
                    oh_g[LANES * (side * EB + k) : LANES * (side * EB + k + 1), :] = one_hot(
                        grad_columns[LANES * k : LANES * (k + 1), 1 - side : 2 - side]
                    )
            masks(qm_g, gc, 2 * EB, NG)
        arrived(back)
        tiles = [edge_tile(back, 0, t, True) for t in range(3)]
        for k in range(EB):
            remain = res[k] - image_block(tiles, k)
            new_step = rho_next * rho_now * step[k] + (2.0 * rho_next / spread) * remain * recip[k]
            step[k] = new_step
            ve[k] = ve[k] + new_step
        extend = back + 1
        for t in range(3):
            send_bufs[extend][t, 0] = pick(ve, sr, sc, t, EB)
            launch(extend, t)
        rho_now = rho_next
    back = X_CHEB + 4
    stiff_image(extend, back)
    arrived(X_NDIAG)
    tiles = [node_tile(X_NDIAG, n, True) for n in range(2)]
    for k in range(NB):
        nrecip[k] = 1.0 / (nrecip[k] + returned(inv_n, tiles, k, 4))
    arrived(back)
    tiles = [edge_tile(back, 0, t, True) for t in range(3)]
    for k in range(EB):
        after = split(res[k] - image_block(tiles, k))
        st[0:16, LANES * k : LANES * (k + 1)] = after
        st[0:16, LANES * (EB + k) : LANES * (EB + k + 1)] = -after

    def node_return(e, qm, width, table, blocks):
        fill(0, qm, NB, NG, blocks, 0)
        product = scatter(32, width, table)
        for t in range(3):
            send_bufs[e][t, 0] = joined(product, t // 2)
            launch(e, t)
        fill(0, qm, 0, NB, blocks, 0)
        product = scatter(48, width, table)
        for k in range(NB):
            ntot[k] = joined(product, k)

    def node_sum(e):
        arrived(e)
        tiles = [node_tile(e, n, True) for n in range(2)]
        return [ntot[k] + returned(inv_n, tiles, k, 4) for k in range(NB)]

    def node_send(e):
        picked = [pick(ne, tr, tc, n, NB) for n in range(2)]
        for t in range(3):
            send_bufs[e][t, 0] = picked[t // 2]
            launch(e, t)

    def node_ghosts(e):
        arrived(e)
        for n in range(2):
            ne[NB + n] = node_tile(e, n, False)

    node_return(X_NODE, qm_g, GCOL, oh_g, 2 * EB)

    gather([vp], er, ec, 2 * EDOF, [pe], 0, EG, 4)

    def p_consume(store):
        def consume(i, total, carry):
            keep_terms(None, store, 0, i, total)
            return carry

        return consume

    lax.fori_loop(0, 5, apply(stiff_ref, vp, EDOF, 4, p_consume(32)), 0)

    for k, total in enumerate(node_sum(X_NODE)):
        nres[k] = total
        first = jacobi_weight * total * nrecip[k]
        nfirst[k] = first
        ne[k] = first
    node_send(X_NODE + 1)
    gather([nv], nr, nc, 2 * NDOF, [ne], 0, NB, 4)
    lax.fori_loop(0, 5, apply(mass_ref, vp, EDOF, 4, p_consume(48)), 0)
    node_ghosts(X_NODE + 1)
    gather([nv], nr, nc, 2 * NDOF, [ne], NB, NG, 4)

    def node_consume(i, total, carry):
        st[pl.ds(0, 16), cols(i * LANES)] = split(total)
        return carry

    lax.fori_loop(0, 5, apply(nodal_ref, nv, NDOF, 2, node_consume), 0)
    node_return(X_NODE + 2, qm_n, NCOL, oh_n, 2 * NDOF)

    def keep_basis(values, base):
        def body(i, carry):
            basis_t[pl.ds(base, 16), cols(i * LANES)] = split(values[i])
            return carry

        lax.fori_loop(0, 2 * EDOF, body, 0, unroll=4)

    keep_basis(vx, 0)
    keep_basis(vp, 32)
    for k, total in enumerate(node_sum(X_NODE + 2)):
        ne[k] = nfirst[k] + jacobi_weight * (nres[k] - total) * nrecip[k]
    node_send(X_NODE + 3)
    gather([gv], gr, gc, 2 * EB, [ne], 0, NB, 4)
    node_ghosts(X_NODE + 3)
    gather([gv], gr, gc, 2 * EB, [ne], NB, NG, 4)
    for k in range(EB):
        total = ve[k] + gv[k] - gv[EB + k]
        ve[k] = total
        w_ref[:, LANES * k : LANES * (k + 1)] = total

    for t in range(3):
        send_bufs[X_W][t, 0] = pick(ve, sr, sc, t, EB)
        launch(X_W, t)
    image_t[96:128, :] = jnp.zeros((32, ECOL), bf16)
    gather([vv], er, ec, 2 * EDOF, [ve], 0, EB, 4)
    arrived(X_W)
    for t in range(3):
        ve[EB + t] = edge_tile(X_W, 0, t, False)
    gather([vv], er, ec, 2 * EDOF, [ve], EB, EG, 4)
    lax.fori_loop(0, 5, apply(stiff_ref, vv, EDOF, 4, p_consume(64)), 0)
    lax.fori_loop(0, 5, apply(mass_ref, vv, EDOF, 4, p_consume(80)), 0)
    keep_basis(vv, 16)
    product = lax.dot_general(
        basis_t[...], image_t[...], (((1,), (1,)), ((), ())), preferred_element_type=f32
    )

    def basis_rows(b):
        rows = joined(product, b)
        return rows + pltpu.roll(rows, LANES - 8, 1)

    x_rows, w_rows, p_rows = basis_rows(0), basis_rows(1), basis_rows(2)
    even = lane8 % 16 < 8
    packed = jnp.where(
        lane8 < 96,
        jnp.where(even, w_rows, pltpu.roll(x_rows, 8, 1)),
        jnp.where(even, pltpu.roll(p_rows, 64, 1), pltpu.roll(p_rows, 40, 1)),
    )
    reduce_start(2, 0, packed)
    reduce_start(3, 1, reduce_finish(2, 0))
    full = reduce_finish(3, 1) * (1.0 / (devices * LANES * EB))
    turned = full.T
    for m, out in enumerate((gram_s_ref, gram_m_ref)):

        def piece(at):
            return full[:, at : at + 8]

        xs, ps, ws = 16 * m, 32 + 16 * m, 64 + 16 * m
        upper = jnp.concatenate([piece(xs + 8), piece(ws + 8), piece(ps + 8)], axis=1)
        middle = jnp.concatenate([piece(xs), piece(ws), piece(ps)], axis=1)
        lower = jnp.concatenate(
            [turned[ps + 8 : ps + 16, :], piece(104 + 16 * m), piece(96 + 16 * m)], axis=1
        )
        out[...] = jnp.concatenate([upper, middle, lower], axis=0)

    for e in range(len(COUNTS)):
        whole(e).wait_send()
    for slot in range(4):
        reduce_whole(slot, slot % 2).wait_send()


def solution(mesh):
    devices = mesh.shape["dom"]

    def shards(*arrays):
        def tiles(*lead):
            return pltpu.VMEM((*lead, 8, LANES), f32)

        def integers(count):
            return pltpu.VMEM((count, 8, LANES), jnp.int32)

        def halves(rows, width):
            return pltpu.VMEM((rows, width), bf16)

        scratch = [
            tiles(EG),
            tiles(EG),
            tiles(EG),
            tiles(NG),
            tiles(2 * EDOF),
            tiles(2 * EDOF),
            tiles(2 * EDOF),
            tiles(2 * NDOF),
            tiles(2 * EB),
            integers(2 * EDOF),
            integers(2 * EDOF),
            integers(2 * NDOF),
            integers(2 * NDOF),
            integers(2 * EB),
            integers(2 * EB),
            integers(3),
            integers(3),
            integers(2),
            integers(2),
            integers(6 * EB),
            integers(6 * NB),
            halves(ECOL, LANES),
            halves(16 * EG, ECOL),
            halves(NCOL, LANES),
            halves(16 * NG, NCOL),
            halves(GCOL, LANES),
            halves(16 * NG, GCOL),
            halves(32, ECOL),
            halves(32 * EB, ECOL),
            halves(48, ECOL),
            halves(128, ECOL),
            tiles(EB),
            tiles(EB),
            tiles(EB),
            tiles(EB),
            tiles(EB),
            tiles(NB),
            tiles(NB),
            tiles(NB),
            tiles(NB),
            [tiles(3, count) for count in COUNTS],
            [tiles(6, count) for count in COUNTS],
            tiles(4),
            tiles(4, max(LOW, devices // LOW)),
            pltpu.SemaphoreType.DMA((len(COUNTS),)),
            pltpu.SemaphoreType.DMA((len(COUNTS),)),
            pltpu.SemaphoreType.DMA((4,)),
            pltpu.SemaphoreType.DMA((4,)),
        ]
        vmem = pl.BlockSpec(memory_space=pltpu.VMEM)
        return pl.pallas_call(
            lambda *refs: kernel(devices, *refs),
            out_shape=(
                jax.ShapeDtypeStruct((8, LANES * EB), f32),
                jax.ShapeDtypeStruct((24, 24), f32),
                jax.ShapeDtypeStruct((24, 24), f32),
            ),
            in_specs=[vmem] * 10,
            out_specs=(vmem, vmem, vmem),
            scratch_shapes=scratch,
            compiler_params=pltpu.CompilerParams(
                collective_id=0, has_side_effects=True, vmem_limit_bytes=56 * 1024 * 1024
            ),
        )(*arrays)

    split_last = P(None, "dom")
    matrices = P(None, None, "dom")
    in_specs = (split_last,) * 2 + (matrices,) * 3 + (split_last,) * 5
    out_specs = (split_last, P(), P())
    return jax.shard_map(shards, mesh=mesh, in_specs=in_specs, out_specs=out_specs, check_vma=False)
```

```python
import jax
import jax.numpy as jnp
from jax import lax
from jax.experimental import pallas as pl
from jax.experimental.pallas import tpu as pltpu
from jax.sharding import PartitionSpec as P

CHEB_DEG = 3
OFFSETS = (1, 4, 16)
LOW = 16
LANES = 128
EDOF = 20
NDOF = 10
EB = 12
EG = 15
NB = 3
NG = 6
ECOL = EDOF * 256
NCOL = NDOF * 256
GCOL = 2 * 1536
interval_low = 0.3
interval_high = 1.7
jacobi_weight = 0.7

f32 = jnp.float32
bf16 = jnp.bfloat16
MESH = pl.DeviceIdType.MESH

PAIRS = [(a, b) for a in range(6) for b in range(a, 6) if b != a ^ 1]
X_PAIR, X_LINK, X_RETURN, X_W = 0, 1, 2, 3
PLAIN = (2, 2, 1, 1)
M_DIAG, M_IMAGE, M_CHEB, M_NDIAG, M_NODE = 0, 1, 2, 4, 5
MERGED = (1, 2, 1, 1, 1, 1, 1)


def take(values, lanes):
    return jnp.take_along_axis(values, lanes, axis=1)


def split(values):
    high = values.astype(bf16).astype(f32)
    return jnp.concatenate([high, values - high], axis=0).astype(bf16)


def spread_row(row):
    return jnp.broadcast_to(row, (8, row.shape[1]))


def cols(start, size=LANES):
    return pl.ds(pl.multiple_of(start, LANES), size)


def kernel(
    devices,
    x_ref,
    p_ref,
    stiff_hbm,
    mass_hbm,
    nodal_hbm,
    elem_edge_ref,
    elem_node_ref,
    send_edge_ref,
    send_node_ref,
    grad_ref,
    w_ref,
    gram_s_ref,
    gram_m_ref,
    stiff_ref,
    mass_ref,
    nodal_ref,
    xe,
    pe,
    ve,
    ne,
    vx,
    vp,
    vv,
    nv,
    gv,
    er,
    ec,
    nr,
    nc,
    gr,
    gc,
    sr,
    sc,
    tr,
    tc,
    inv_e,
    inv_n,
    link_e,
    link_n,
    oh_e,
    qm_e,
    oh_n,
    qm_n,
    oh_g,
    qm_g,
    st,
    left,
    basis_t,
    image_t,
    tot,
    tot2,
    res,
    recip,
    step,
    nres,
    nrecip,
    nfirst,
    ntot,
    send_bufs,
    recv_bufs,
    near_send,
    near_recv,
    far_send,
    far_recv,
    ar_send,
    ar_recv,
    load_sems,
    send_sems,
    recv_sems,
    near_send_sems,
    near_recv_sems,
    far_send_sems,
    far_recv_sems,
    ar_send_sems,
    ar_recv_sems,
):
    loads = [
        pltpu.make_async_copy(source, target, load_sems.at[i])
        for i, (source, target) in enumerate(
            ((stiff_hbm, stiff_ref), (mass_hbm, mass_ref), (nodal_hbm, nodal_ref))
        )
    ]
    for load in loads:
        load.start()
    me = lax.axis_index("dom")
    low, high = lax.rem(me, LOW), lax.div(me, LOW)
    highs = devices // LOW
    around = []
    for offset in OFFSETS:
        around.append(lax.rem(me + offset, devices))
        around.append(lax.rem(me + devices - offset, devices))
    signed = [o * s for o in OFFSETS for s in (1, -1)]
    beyond = [lax.rem(me + 2 * devices - signed[a] - signed[b], devices) for a, b in PAIRS]
    groups = [
        [high * LOW + lax.rem(low + m, LOW) for m in range(1, LOW)],
        [lax.rem(high + m, highs) * LOW + low for m in range(1, highs)],
    ]

    barrier = pltpu.get_barrier_semaphore()
    everyone = around + beyond + groups[0] + groups[1]
    for partner in everyone:
        pl.semaphore_signal(barrier, inc=1, device_id=(partner,), device_id_type=MESH)

    lane8 = lax.broadcasted_iota(jnp.int32, (8, LANES), 1)
    row8 = lax.broadcasted_iota(jnp.int32, (8, LANES), 0)
    first_half = lane8 < 64
    lane128 = lax.broadcasted_iota(jnp.int32, (LANES, LANES), 1).astype(f32)
    zero8 = jnp.zeros((8, LANES), f32)

    def launch(e, t):
        for side in range(2):
            pltpu.make_async_remote_copy(
                src_ref=send_bufs[e].at[t],
                dst_ref=recv_bufs[e].at[2 * t + side],
                send_sem=send_sems.at[e],
                recv_sem=recv_sems.at[e],
                device_id=(around[2 * t + side],),
                device_id_type=MESH,
            ).start()

    def whole(e):
        return pltpu.make_async_remote_copy(
            src_ref=recv_bufs[e],
            dst_ref=recv_bufs[e],
            send_sem=send_sems.at[e],
            recv_sem=recv_sems.at[e],
            device_id=(around[0],),
            device_id_type=MESH,
        )

    def arrived(e):
        whole(e).wait_recv()

    def edge_tile(e, i, t, back):
        first, second = (2 * t + 1, 2 * t) if back else (2 * t, 2 * t + 1)
        return jnp.where(first_half, recv_bufs[e][first, i], recv_bufs[e][second, i])

    def far_start(e, ghosts):
        for i, tiles in enumerate(ghosts):
            turned = [pltpu.roll(tile, 64, 1) for tile in tiles]
            for n, (a, b) in enumerate(PAIRS):
                front = (turned if a % 2 else tiles)[a // 2]
                rear = (tiles if b % 2 else turned)[b // 2]
                far_send[e][n, i] = front if a == b else jnp.where(first_half, front, rear)
        for n in range(len(PAIRS)):
            pltpu.make_async_remote_copy(
                src_ref=far_send[e].at[n],
                dst_ref=far_recv[e].at[n],
                send_sem=far_send_sems.at[e],
                recv_sem=far_recv_sems.at[e],
                device_id=(beyond[n],),
                device_id_type=MESH,
            ).start()

    def near_start(e, owned, ghosts):
        for t in range(3):
            for i in range(len(owned)):
                near_send[e][2 * t, i] = jnp.where(first_half, owned[i][t], ghosts[i][t])
                near_send[e][2 * t + 1, i] = jnp.where(first_half, ghosts[i][t], owned[i][t])
            for side in range(2):
                pltpu.make_async_remote_copy(
                    src_ref=near_send[e].at[2 * t + side],
                    dst_ref=near_recv[e].at[2 * t + side],
                    send_sem=near_send_sems.at[e],
                    recv_sem=near_recv_sems.at[e],
                    device_id=(around[2 * t + side],),
                    device_id_type=MESH,
                ).start()

    def near_whole(e):
        return pltpu.make_async_remote_copy(
            src_ref=near_recv[e],
            dst_ref=near_recv[e],
            send_sem=near_send_sems.at[e],
            recv_sem=near_recv_sems.at[e],
            device_id=(around[0],),
            device_id_type=MESH,
        )

    def far_whole(e):
        return pltpu.make_async_remote_copy(
            src_ref=far_recv[e],
            dst_ref=far_recv[e],
            send_sem=far_send_sems.at[e],
            recv_sem=far_recv_sems.at[e],
            device_id=(around[0],),
            device_id_type=MESH,
        )

    def slot_of(held, other):
        pair = (min(held, other), max(held, other))
        return PAIRS.index(pair), (0 if held <= other else 1)

    def make_links(links, i):
        for t in range(3):
            places = edge_tile(X_LINK, i, t, False).astype(jnp.int32)
            for d in range(6):
                place = spread_row(places[d : d + 1])
                lower = None if d == 2 * t else slot_of(d, 2 * t + 1)[1]
                upper = None if d == 2 * t + 1 else slot_of(d, 2 * t)[1]
                low_at = jnp.zeros_like(place) if lower is None else LANES + 64 * lower + (place & 63)
                up_at = jnp.zeros_like(place) if upper is None else LANES + 64 * upper + (place & 63)
                links[t * 6 + d] = jnp.where(place >= LANES, jnp.where(first_half, low_at, up_at), 0)

    def finish_merge(e, totals, links, inverse, owned):
        near_whole(e).wait_recv()
        for i, total in enumerate(totals):
            back = [jnp.where(first_half, near_recv[e][2 * t + 1, i], near_recv[e][2 * t, i]) for t in range(3)]
            for k in range(owned):
                total[k] = total[k] + returned(inverse, back, k)
        far_whole(e).wait_recv()
        for i, total in enumerate(totals):
            for t in range(3):
                value = total[owned + t] + jnp.where(
                    first_half, near_recv[e][2 * t, i], near_recv[e][2 * t + 1, i]
                )
                for d in range(6):
                    at = links[t * 6 + d]
                    sources = []
                    if d != 2 * t:
                        sources.append(far_recv[e][slot_of(d, 2 * t + 1)[0], i])
                    if d != 2 * t + 1:
                        sources.append(far_recv[e][slot_of(d, 2 * t)[0], i])
                    found = [take(source, at & 127) for source in sources]
                    term = found[0] if len(found) == 1 else jnp.where(first_half, found[0], found[1])
                    value = value + jnp.where(at >= LANES, term, 0.0)
                total[owned + t] = value

    def reduce_start(slot, stage, tile):
        mine = (low, high)[stage]
        ar_send[slot] = tile
        ar_recv[slot, mine] = tile
        for partner in groups[stage]:
            pltpu.make_async_remote_copy(
                src_ref=ar_send.at[slot],
                dst_ref=ar_recv.at[slot, mine],
                send_sem=ar_send_sems.at[slot],
                recv_sem=ar_recv_sems.at[slot],
                device_id=(partner,),
                device_id_type=MESH,
            ).start()

    def reduce_whole(slot, stage):
        part = ar_recv.at[slot, pl.ds(0, (LOW, highs)[stage] - 1)]
        return pltpu.make_async_remote_copy(
            src_ref=part,
            dst_ref=part,
            send_sem=ar_send_sems.at[slot],
            recv_sem=ar_recv_sems.at[slot],
            device_id=(around[0],),
            device_id_type=MESH,
        )

    def reduce_finish(slot, stage):
        reduce_whole(slot, stage).wait_recv()
        parts = [ar_recv[slot, i] for i in range((LOW, highs)[stage])]
        while len(parts) > 1:
            parts = [a + b for a, b in zip(parts[::2], parts[1::2])]
        return parts[0]

    def gather(out, lanes, blocks, count, sources, first, last, unroll):
        def body(i, carry):
            r, c = lanes[i], blocks[i]
            for o, s in zip(out, sources):
                value = zero8 if first == 0 else o[i]
                for k in range(first, last):
                    value = jnp.where(c == k, take(s[k], r), value)
                o[i] = value
            return carry

        lax.fori_loop(0, count, body, 0, unroll=unroll)

    def pick(source, lanes, blocks, t, owned):
        value = zero8
        for k in range(owned):
            value = jnp.where(blocks[t] == k, take(source[k], lanes[t]), value)
        return value

    def returned(inverse, tiles, block):
        value = None
        for d in range(6):
            where = inverse[block * 6 + d]
            term = jnp.where(where >= LANES, take(tiles[d // 2], where & 127), 0.0)
            value = term if value is None else value + term
        return value

    def index_tables(row, lanes, blocks, i):
        lanes[i] = spread_row(row & 127)
        blocks[i] = spread_row(row >> 7)

    def masks(qm, blocks, count, parts):
        def body(i, carry):
            c = blocks[i]
            for q in range(parts):
                one = jnp.where(c == q, 1.0, 0.0)
                qm[pl.ds(16 * q, 16), cols(i * LANES)] = jnp.concatenate([one, one], 0).astype(bf16)
            return carry

        lax.fori_loop(0, count, body, 0, unroll=2)

    def one_hot(column):
        return jnp.where(jnp.broadcast_to(column, (LANES, LANES)) == lane128, 1.0, 0.0).astype(bf16)

    def columns_of(rows):
        count, width = rows.shape
        padded = -count % 8
        if padded:
            rows = jnp.concatenate([rows, jnp.zeros((padded, width), jnp.int32)], axis=0)
        return (rows & 127).astype(f32).T

    def fill(base, qm, first, last, count, source, unroll=2):
        def body(i, carry):
            term = st[pl.ds(source, 16), cols(i * LANES)]
            for q in range(first, last):
                left[pl.ds(base + 16 * (q - first), 16), cols(i * LANES)] = (
                    term * qm[pl.ds(16 * q, 16), cols(i * LANES)]
                )
            return carry

        lax.fori_loop(0, count, body, 0, unroll=unroll)

    def scatter(rows, width, table):
        return jnp.dot(left[0:rows, 0:width], table[...], preferred_element_type=f32)

    def joined(product, q):
        return product[16 * q : 16 * q + 8] + product[16 * q + 8 : 16 * q + 16]

    def apply(matrix, values, size, group, consume):
        def body(jj, carry):
            for h in range(2):
                total = [None] * group
                for k in range(size):
                    value = values[2 * k + h]
                    for u in range(group):
                        row = matrix[jj * group + u, pl.ds(k, 1), pl.ds(LANES * h, LANES)]
                        term = row * value
                        total[u] = term if k == 0 else total[u] + term
                for u in range(group):
                    carry = consume(2 * (jj * group + u) + h, total[u], carry)
            return carry

        return body

    def shared_rows(ref, width):
        rows = []
        for t in range(3):
            pieces = []
            for d in (2 * t, 2 * t + 1):
                pieces.append(ref[d : d + 1, :])
                if width < 64:
                    pieces.append(jnp.full((1, 64 - width), -LANES, jnp.int32))
            rows.append(jnp.concatenate(pieces, axis=1))
        return rows

    edge_rows = shared_rows(send_edge_ref, 64)
    for t in range(3):
        index_tables(edge_rows[t], sr, sc, t)
    for k in range(EB):
        xe[k] = x_ref[:, LANES * k : LANES * (k + 1)]
        pe[k] = p_ref[:, LANES * k : LANES * (k + 1)]
    for t in range(3):
        send_bufs[X_PAIR][t, 0] = pick(xe, sr, sc, t, EB)
        send_bufs[X_PAIR][t, 1] = pick(pe, sr, sc, t, EB)
    pl.semaphore_wait(barrier, len(everyone))
    for t in range(3):
        launch(X_PAIR, t)

    for j in range(EDOF):
        for h in range(2):
            row = elem_edge_ref[j : j + 1, LANES * h : LANES * (h + 1)]
            index_tables(row, er, ec, 2 * j + h)
    edge_columns = columns_of(elem_edge_ref[...])
    for j in range(EDOF):
        for h in range(2):
            oh_e[256 * j + LANES * h : 256 * j + LANES * (h + 1), :] = one_hot(
                edge_columns[LANES * h : LANES * (h + 1), j : j + 1]
            )
    masks(qm_e, ec, 2 * EDOF, EG)

    loads[0].wait()
    for j in range(EDOF):
        for h in range(2):
            diagonal = spread_row(stiff_ref[j, j : j + 1, LANES * h : LANES * (h + 1)])
            st[0:16, 256 * j + LANES * h : 256 * j + LANES * (h + 1)] = split(diagonal)
    fill(0, qm_e, 0, EG, 2 * EDOF, 0)
    product = scatter(16 * EG, ECOL, oh_e)
    for k in range(EG):
        recip[k] = joined(product, k)

    def merge_start(e, totals, lanes, blocks, owned):
        ghosts = [[total[owned + t] for t in range(3)] for total in totals]
        far_start(e, ghosts)
        shares = [[pick(total, lanes, blocks, t, owned) for t in range(3)] for total in totals]
        near_start(e, shares, ghosts)

    merge_start(M_DIAG, [recip], sr, sc, EB)

    gather([vx], er, ec, 2 * EDOF, [xe], 0, EB, 4)

    def inverse_lists(inverse, rows, lanes, blocks, owned, i):
        turned = columns_of(jnp.concatenate(rows, axis=0))
        table = jnp.concatenate([one_hot(turned[:, t : t + 1]) for t in range(3)], axis=0)
        parts = []
        for q in range(0, owned + owned % 2):
            line = []
            for t in range(3):
                keep = jnp.logical_and(row8 == 2 * t + (lane8 >> 6), blocks[t] == q)
                line.append(jnp.where(keep, LANES + lane8, 0).astype(f32))
            parts.append(jnp.concatenate(line, axis=1))
        found = jnp.dot(
            jnp.concatenate(parts, axis=0).astype(bf16), table, preferred_element_type=f32
        )
        places = [found[8 * q : 8 * q + 8] for q in range(owned)]
        for t in range(3):
            send_bufs[X_LINK][t, i] = pick(places, lanes, blocks, t, owned)
        for q in range(owned):
            place = places[q].astype(jnp.int32)
            for d in range(6):
                inverse[q * 6 + d] = spread_row(place[d : d + 1])

    inverse_lists(inv_e, edge_rows, sr, sc, EB, 0)
    node_rows = shared_rows(send_node_ref, 32)
    for t in range(3):
        index_tables(node_rows[t], tr, tc, t)
    inverse_lists(inv_n, node_rows, tr, tc, NB, 1)
    for t in range(3):
        launch(X_LINK, t)

    arrived(X_PAIR)
    for t in range(3):
        xe[EB + t] = edge_tile(X_PAIR, 0, t, False)
        pe[EB + t] = edge_tile(X_PAIR, 1, t, False)
    gather([vx], er, ec, 2 * EDOF, [xe], EB, EG, 4)

    def keep_terms(base, store, ghost_base, i, total):
        term = split(total)
        place = cols(i * LANES)
        if store is not None:
            image_t[pl.ds(store, 16), place] = term
        if base is not None:
            st[pl.ds(base, 16), place] = term
            for q in range(EB, EG):
                left[pl.ds(ghost_base + 16 * (q - EB), 16), place] = term * qm_e[pl.ds(16 * q, 16), place]

    def x_consume(base, store, ghost_base):
        def consume(i, total, carry):
            keep_terms(base, store, ghost_base, i, total)
            return carry + total * vx[i]

        return consume

    loads[1].wait()
    numerator = lax.fori_loop(0, 5, apply(stiff_ref, vx, EDOF, 4, x_consume(0, 0, 0)), zero8)
    denominator = lax.fori_loop(0, 5, apply(mass_ref, vx, EDOF, 4, x_consume(16, 16, 48)), zero8)
    numerator = jnp.sum(numerator, axis=1, keepdims=True)
    denominator = jnp.sum(denominator, axis=1, keepdims=True)
    reduce_start(0, 0, jnp.where(lane8 == 0, numerator, jnp.where(lane8 == 1, denominator, 0.0)))
    product = scatter(96, ECOL, oh_e)
    ghosts = [[joined(product, 3 * i + t) for t in range(3)] for i in range(2)]
    far_start(M_IMAGE, ghosts)
    for t in range(3):
        tot[EB + t] = ghosts[0][t]
        tot2[EB + t] = ghosts[1][t]
    fill(0, qm_e, 0, EB, 2 * EDOF, 0)
    fill(16 * EB, qm_e, 0, EB, 2 * EDOF, 16)
    product = scatter(32 * EB, ECOL, oh_e)
    for k in range(EB):
        tot[k] = joined(product, k)
        tot2[k] = joined(product, EB + k)
    near_start(
        M_IMAGE,
        [[pick(total, sr, sc, t, EB) for t in range(3)] for total in (tot, tot2)],
        [[total[EB + t] for t in range(3)] for total in (tot, tot2)],
    )
    center = 0.5 * (interval_high + interval_low)
    spread = 0.5 * (interval_high - interval_low)
    arrived(X_LINK)
    make_links(link_e, 0)
    make_links(link_n, 1)
    reduce_start(1, 1, reduce_finish(0, 0))
    finish_merge(M_DIAG, [recip], link_e, inv_e, EB)
    for k in range(EG):
        recip[k] = 1.0 / recip[k]

    def padded(index):
        ghost = index - LANES * NB
        return jnp.where(ghost < 0, index, LANES * NB + ((ghost >> 5) << 6) + (ghost & 31))

    for j in range(NDOF):
        for h in range(2):
            row = padded(elem_node_ref[j : j + 1, LANES * h : LANES * (h + 1)])
            index_tables(row, nr, nc, 2 * j + h)
    node_columns = columns_of(padded(elem_node_ref[...]))
    for j in range(NDOF):
        for h in range(2):
            oh_n[256 * j + LANES * h : 256 * j + LANES * (h + 1), :] = one_hot(
                node_columns[LANES * h : LANES * (h + 1), j : j + 1]
            )
    masks(qm_n, nc, 2 * NDOF, NG)

    finish_merge(M_IMAGE, [tot, tot2], link_e, inv_e, EB)
    sums = reduce_finish(1, 1)
    quotient = jnp.broadcast_to(sums[:, 0:1] / sums[:, 1:2], (8, LANES))
    for k in range(EG):
        residual = tot[k] - quotient * tot2[k]
        res[k] = residual
        first_step = residual * recip[k] * (1.0 / center)
        step[k] = first_step
        ve[k] = first_step

    def stiff_terms():
        gather([vv], er, ec, 2 * EDOF, [ve], 0, EG, 8)

        def consume(i, total, carry):
            keep_terms(0, None, 0, i, total)
            return carry

        lax.fori_loop(0, 5, apply(stiff_ref, vv, EDOF, 4, consume), 0)
        product = scatter(48, ECOL, oh_e)
        return [joined(product, t) for t in range(3)]

    def stiff_owned():
        fill(0, qm_e, 0, EB, 2 * EDOF, 0)
        product = scatter(16 * EB, ECOL, oh_e)
        for k in range(EB):
            tot[k] = joined(product, k)

    sigma = center / spread
    rho_now = 1.0 / sigma
    for turn in range(CHEB_DEG - 1):
        rho_next = 1.0 / (2.0 * sigma - rho_now)
        ghosts = stiff_terms()
        far_start(M_CHEB + turn, [ghosts])
        for t in range(3):
            tot[EB + t] = ghosts[t]
        stiff_owned()
        near_start(
            M_CHEB + turn,
            [[pick(tot, sr, sc, t, EB) for t in range(3)]],
            [[tot[EB + t] for t in range(3)]],
        )
        if turn == 0:
            loads[2].wait()
            for j in range(NDOF):
                for h in range(2):
                    diagonal = spread_row(nodal_ref[j, j : j + 1, LANES * h : LANES * (h + 1)])
                    st[0:16, 256 * j + LANES * h : 256 * j + LANES * (h + 1)] = split(diagonal)
            fill(0, qm_n, 0, NG, 2 * NDOF, 0)
            product = scatter(16 * NG, NCOL, oh_n)
            for k in range(NG):
                nrecip[k] = joined(product, k)
            merge_start(M_NDIAG, [nrecip], tr, tc, NB)
        else:
            for side in range(2):
                for k in range(EB):
                    row = padded(grad_ref[1 - side : 2 - side, LANES * k : LANES * (k + 1)])
                    index_tables(row, gr, gc, side * EB + k)
            grad_columns = columns_of(padded(grad_ref[...]))
            for side in range(2):
                for k in range(EB):
                    oh_g[LANES * (side * EB + k) : LANES * (side * EB + k + 1), :] = one_hot(
                        grad_columns[LANES * k : LANES * (k + 1), 1 - side : 2 - side]
                    )
            masks(qm_g, gc, 2 * EB, NG)
        finish_merge(M_CHEB + turn, [tot], link_e, inv_e, EB)
        for k in range(EG):
            remain = res[k] - tot[k]
            new_step = rho_next * rho_now * step[k] + (2.0 * rho_next / spread) * remain * recip[k]
            step[k] = new_step
            ve[k] = ve[k] + new_step
        rho_now = rho_next
    ghosts = stiff_terms()
    for t in range(3):
        send_bufs[X_RETURN][t, 0] = ghosts[t]
        launch(X_RETURN, t)
    stiff_owned()
    finish_merge(M_NDIAG, [nrecip], link_n, inv_n, NB)
    for k in range(NG):
        padding = jnp.logical_and(k >= NB, (lane8 & 63) >= 32)
        nrecip[k] = 1.0 / jnp.where(padding, 1.0, nrecip[k])
    arrived(X_RETURN)
    tiles = [edge_tile(X_RETURN, 0, t, True) for t in range(3)]
    for k in range(EB):
        after = split(res[k] - (tot[k] + returned(inv_e, tiles, k)))
        st[0:16, LANES * k : LANES * (k + 1)] = after
        st[0:16, LANES * (EB + k) : LANES * (EB + k + 1)] = -after

    def node_start(e, qm, width, table, blocks):
        fill(0, qm, 0, NG, blocks, 0)
        product = scatter(16 * NG, width, table)
        for k in range(NG):
            ntot[k] = joined(product, k)
        merge_start(e, [ntot], tr, tc, NB)

    node_start(M_NODE, qm_g, GCOL, oh_g, 2 * EB)

    gather([vp], er, ec, 2 * EDOF, [pe], 0, EG, 8)

    def p_consume(store):
        def consume(i, total, carry):
            keep_terms(None, store, 0, i, total)
            return carry

        return consume

    lax.fori_loop(0, 5, apply(stiff_ref, vp, EDOF, 4, p_consume(32)), 0)
    lax.fori_loop(0, 5, apply(mass_ref, vp, EDOF, 4, p_consume(48)), 0)
    finish_merge(M_NODE, [ntot], link_n, inv_n, NB)
    for k in range(NG):
        nres[k] = ntot[k]
        first = jacobi_weight * ntot[k] * nrecip[k]
        nfirst[k] = first
        ne[k] = first
    gather([nv], nr, nc, 2 * NDOF, [ne], 0, NG, 4)

    def node_consume(i, total, carry):
        st[pl.ds(0, 16), cols(i * LANES)] = split(total)
        return carry

    lax.fori_loop(0, 5, apply(nodal_ref, nv, NDOF, 2, node_consume), 0)
    node_start(M_NODE + 1, qm_n, NCOL, oh_n, 2 * NDOF)

    def keep_basis(values, base):
        def body(i, carry):
            basis_t[pl.ds(base, 16), cols(i * LANES)] = split(values[i])
            return carry

        lax.fori_loop(0, 2 * EDOF, body, 0, unroll=4)

    keep_basis(vx, 0)
    keep_basis(vp, 32)
    finish_merge(M_NODE + 1, [ntot], link_n, inv_n, NB)
    for k in range(NG):
        ne[k] = nfirst[k] + jacobi_weight * (nres[k] - ntot[k]) * nrecip[k]
    gather([gv], gr, gc, 2 * EB, [ne], 0, NG, 4)
    for k in range(EB):
        total = ve[k] + gv[k] - gv[EB + k]
        ve[k] = total
        w_ref[:, LANES * k : LANES * (k + 1)] = total

    for t in range(3):
        send_bufs[X_W][t, 0] = pick(ve, sr, sc, t, EB)
        launch(X_W, t)
    image_t[96:128, :] = jnp.zeros((32, ECOL), bf16)
    gather([vv], er, ec, 2 * EDOF, [ve], 0, EB, 4)
    arrived(X_W)
    for t in range(3):
        ve[EB + t] = edge_tile(X_W, 0, t, False)
    gather([vv], er, ec, 2 * EDOF, [ve], EB, EG, 4)
    lax.fori_loop(0, 5, apply(stiff_ref, vv, EDOF, 4, p_consume(64)), 0)
    lax.fori_loop(0, 5, apply(mass_ref, vv, EDOF, 4, p_consume(80)), 0)
    keep_basis(vv, 16)
    product = lax.dot_general(
        basis_t[...], image_t[...], (((1,), (1,)), ((), ())), preferred_element_type=f32
    )

    def basis_rows(b):
        rows = joined(product, b)
        return rows + pltpu.roll(rows, LANES - 8, 1)

    x_rows, w_rows, p_rows = basis_rows(0), basis_rows(1), basis_rows(2)
    even = lane8 % 16 < 8
    packed = jnp.where(
        lane8 < 96,
        jnp.where(even, w_rows, pltpu.roll(x_rows, 8, 1)),
        jnp.where(even, pltpu.roll(p_rows, 64, 1), pltpu.roll(p_rows, 40, 1)),
    )
    reduce_start(2, 0, packed)
    reduce_start(3, 1, reduce_finish(2, 0))
    full = reduce_finish(3, 1) * (1.0 / (devices * LANES * EB))
    turned = full.T
    for m, out in enumerate((gram_s_ref, gram_m_ref)):

        def piece(at):
            return full[:, at : at + 8]

        xs, ps, ws = 16 * m, 32 + 16 * m, 64 + 16 * m
        upper = jnp.concatenate([piece(xs + 8), piece(ws + 8), piece(ps + 8)], axis=1)
        middle = jnp.concatenate([piece(xs), piece(ws), piece(ps)], axis=1)
        lower = jnp.concatenate(
            [turned[ps + 8 : ps + 16, :], piece(104 + 16 * m), piece(96 + 16 * m)], axis=1
        )
        out[...] = jnp.concatenate([upper, middle, lower], axis=0)

    for e in range(len(PLAIN)):
        whole(e).wait_send()
    for e in range(len(MERGED)):
        near_whole(e).wait_send()
        far_whole(e).wait_send()
    for slot in range(4):
        reduce_whole(slot, slot % 2).wait_send()


def solution(mesh):
    devices = mesh.shape["dom"]

    def shards(*arrays):
        def tiles(*lead):
            return pltpu.VMEM((*lead, 8, LANES), f32)

        def integers(count):
            return pltpu.VMEM((count, 8, LANES), jnp.int32)

        def halves(rows, width):
            return pltpu.VMEM((rows, width), bf16)

        scratch = [
            pltpu.VMEM(arrays[2].shape, f32),
            pltpu.VMEM(arrays[3].shape, f32),
            pltpu.VMEM(arrays[4].shape, f32),
            tiles(EG),
            tiles(EG),
            tiles(EG),
            tiles(NG),
            tiles(2 * EDOF),
            tiles(2 * EDOF),
            tiles(2 * EDOF),
            tiles(2 * NDOF),
            tiles(2 * EB),
            integers(2 * EDOF),
            integers(2 * EDOF),
            integers(2 * NDOF),
            integers(2 * NDOF),
            integers(2 * EB),
            integers(2 * EB),
            integers(3),
            integers(3),
            integers(3),
            integers(3),
            integers(6 * EB),
            integers(6 * NB),
            integers(18),
            integers(18),
            halves(ECOL, LANES),
            halves(16 * EG, ECOL),
            halves(NCOL, LANES),
            halves(16 * NG, NCOL),
            halves(GCOL, LANES),
            halves(16 * NG, GCOL),
            halves(32, ECOL),
            halves(32 * EB, ECOL),
            halves(48, ECOL),
            halves(128, ECOL),
            tiles(EG),
            tiles(EG),
            tiles(EG),
            tiles(EG),
            tiles(EG),
            tiles(NG),
            tiles(NG),
            tiles(NG),
            tiles(NG),
            [tiles(3, count) for count in PLAIN],
            [tiles(6, count) for count in PLAIN],
            [tiles(6, count) for count in MERGED],
            [tiles(6, count) for count in MERGED],
            [tiles(len(PAIRS), count) for count in MERGED],
            [tiles(len(PAIRS), count) for count in MERGED],
            tiles(4),
            tiles(4, max(LOW, devices // LOW)),
            pltpu.SemaphoreType.DMA((3,)),
            pltpu.SemaphoreType.DMA((len(PLAIN),)),
            pltpu.SemaphoreType.DMA((len(PLAIN),)),
            pltpu.SemaphoreType.DMA((len(MERGED),)),
            pltpu.SemaphoreType.DMA((len(MERGED),)),
            pltpu.SemaphoreType.DMA((len(MERGED),)),
            pltpu.SemaphoreType.DMA((len(MERGED),)),
            pltpu.SemaphoreType.DMA((4,)),
            pltpu.SemaphoreType.DMA((4,)),
        ]
        vmem = pl.BlockSpec(memory_space=pltpu.VMEM)
        return pl.pallas_call(
            lambda *refs: kernel(devices, *refs),
            out_shape=(
                jax.ShapeDtypeStruct((8, LANES * EB), f32),
                jax.ShapeDtypeStruct((24, 24), f32),
                jax.ShapeDtypeStruct((24, 24), f32),
            ),
            in_specs=[vmem] * 2 + [pl.BlockSpec(memory_space=pl.ANY)] * 3 + [vmem] * 5,
            out_specs=(vmem, vmem, vmem),
            scratch_shapes=scratch,
            compiler_params=pltpu.CompilerParams(
                collective_id=0, has_side_effects=True, vmem_limit_bytes=56 * 1024 * 1024
            ),
        )(*arrays)

    split_last = P(None, "dom")
    matrices = P(None, None, "dom")
    in_specs = (split_last,) * 2 + (matrices,) * 3 + (split_last,) * 5
    out_specs = (split_last, P(), P())
    return jax.shard_map(shards, mesh=mesh, in_specs=in_specs, out_specs=out_specs, check_vma=False)
```

```python
import jax
import jax.numpy as jnp
from jax import lax
from jax.experimental import pallas as pl
from jax.experimental.pallas import tpu as pltpu
from jax.sharding import PartitionSpec as P

CHEB_DEG = 3
OFFSETS = (1, 4, 16)
LOW = 16
LANES = 128
EDOF = 20
NDOF = 10
EB = 12
EG = 15
NB = 3
NG = 6
ECOL = EDOF * 256
NCOL = NDOF * 256
GCOL = 2 * 1536
interval_low = 0.3
interval_high = 1.7
jacobi_weight = 0.7

f32 = jnp.float32
bf16 = jnp.bfloat16
MESH = pl.DeviceIdType.MESH

PAIRS = sorted(
    [(a, b) for a in range(6) for b in range(a, 6) if b != a ^ 1],
    key=lambda pair: [(1, 1), (1, 2), (2, 2), (0, 1), (0, 2), (0, 0)].index((pair[0] // 2, pair[1] // 2)),
)
X_PAIR, X_LINK, X_RETURN, X_W = 0, 1, 2, 3
PLAIN = (2, 2, 1, 1)
M_DIAG, M_IMAGE, M_CHEB, M_NDIAG, M_NODE = 0, 1, 2, 4, 5
MERGED = (1, 2, 1, 1, 1, 1, 1)


def take(values, lanes):
    return jnp.take_along_axis(values, lanes, axis=1)


def split(values):
    high = values.astype(bf16).astype(f32)
    return jnp.concatenate([high, values - high], axis=0).astype(bf16)


def spread_row(row):
    return jnp.broadcast_to(row, (8, row.shape[1]))


def cols(start, size=LANES):
    return pl.ds(pl.multiple_of(start, LANES), size)


def kernel(
    devices,
    x_ref,
    p_ref,
    stiff_hbm,
    mass_hbm,
    nodal_hbm,
    elem_edge_ref,
    elem_node_ref,
    send_edge_ref,
    send_node_ref,
    grad_ref,
    w_ref,
    gram_s_ref,
    gram_m_ref,
    stiff_ref,
    mass_ref,
    nodal_ref,
    xe,
    pe,
    ve,
    ne,
    vx,
    vp,
    vv,
    nv,
    gv,
    er,
    ec,
    nr,
    nc,
    gr,
    gc,
    sr,
    sc,
    tr,
    tc,
    inv_e,
    inv_n,
    link_e,
    link_n,
    oh_e,
    qm_e,
    oh_n,
    qm_n,
    oh_g,
    qm_g,
    st,
    left,
    basis_t,
    image_t,
    tot,
    tot2,
    res,
    recip,
    step,
    nres,
    nrecip,
    nfirst,
    ntot,
    send_bufs,
    recv_bufs,
    near_send,
    near_recv,
    far_send,
    far_recv,
    ar_send,
    ar_recv,
    load_sems,
    send_sems,
    recv_sems,
    near_send_sems,
    near_recv_sems,
    far_send_sems,
    far_recv_sems,
    ar_send_sems,
    ar_recv_sems,
):
    loads = [
        pltpu.make_async_copy(source, target, load_sems.at[i])
        for i, (source, target) in enumerate(
            ((stiff_hbm, stiff_ref), (mass_hbm, mass_ref), (nodal_hbm, nodal_ref))
        )
    ]
    for load in loads:
        load.start()
    me = lax.axis_index("dom")
    low, high = lax.rem(me, LOW), lax.div(me, LOW)
    highs = devices // LOW
    around = []
    for offset in OFFSETS:
        around.append(lax.rem(me + offset, devices))
        around.append(lax.rem(me + devices - offset, devices))
    signed = [o * s for o in OFFSETS for s in (1, -1)]
    beyond = [lax.rem(me + 2 * devices - signed[a] - signed[b], devices) for a, b in PAIRS]
    groups = [
        [high * LOW + lax.rem(low + m, LOW) for m in range(1, LOW)],
        [lax.rem(high + m, highs) * LOW + low for m in range(1, highs)],
    ]

    barrier = pltpu.get_barrier_semaphore()
    everyone = around + beyond + groups[0] + groups[1]
    for partner in everyone:
        pl.semaphore_signal(barrier, inc=1, device_id=(partner,), device_id_type=MESH)

    lane8 = lax.broadcasted_iota(jnp.int32, (8, LANES), 1)
    row8 = lax.broadcasted_iota(jnp.int32, (8, LANES), 0)
    first_half = lane8 < 64
    lane128 = lax.broadcasted_iota(jnp.int32, (LANES, LANES), 1).astype(f32)
    zero8 = jnp.zeros((8, LANES), f32)

    def launch(e, t):
        for side in range(2):
            pltpu.make_async_remote_copy(
                src_ref=send_bufs[e].at[t],
                dst_ref=recv_bufs[e].at[2 * t + side],
                send_sem=send_sems.at[e],
                recv_sem=recv_sems.at[e],
                device_id=(around[2 * t + side],),
                device_id_type=MESH,
            ).start()

    def whole(e):
        return pltpu.make_async_remote_copy(
            src_ref=recv_bufs[e],
            dst_ref=recv_bufs[e],
            send_sem=send_sems.at[e],
            recv_sem=recv_sems.at[e],
            device_id=(around[0],),
            device_id_type=MESH,
        )

    def arrived(e):
        whole(e).wait_recv()

    def edge_tile(e, i, t, back):
        first, second = (2 * t + 1, 2 * t) if back else (2 * t, 2 * t + 1)
        return jnp.where(first_half, recv_bufs[e][first, i], recv_bufs[e][second, i])

    def far_start(e, ghosts):
        for i, tiles in enumerate(ghosts):
            turned = [pltpu.roll(tile, 64, 1) for tile in tiles]
            for n, (a, b) in enumerate(PAIRS):
                front = (turned if a % 2 else tiles)[a // 2]
                rear = (tiles if b % 2 else turned)[b // 2]
                far_send[e][n, i] = front if a == b else jnp.where(first_half, front, rear)
        for n in range(len(PAIRS)):
            pltpu.make_async_remote_copy(
                src_ref=far_send[e].at[n],
                dst_ref=far_recv[e].at[n],
                send_sem=far_send_sems.at[e],
                recv_sem=far_recv_sems.at[e],
                device_id=(beyond[n],),
                device_id_type=MESH,
            ).start()

    def near_start(e, owned, ghosts):
        for t in range(3):
            for i in range(len(owned)):
                near_send[e][2 * t, i] = jnp.where(first_half, owned[i][t], ghosts[i][t])
                near_send[e][2 * t + 1, i] = jnp.where(first_half, ghosts[i][t], owned[i][t])
            for side in range(2):
                pltpu.make_async_remote_copy(
                    src_ref=near_send[e].at[2 * t + side],
                    dst_ref=near_recv[e].at[2 * t + side],
                    send_sem=near_send_sems.at[e],
                    recv_sem=near_recv_sems.at[e],
                    device_id=(around[2 * t + side],),
                    device_id_type=MESH,
                ).start()

    def near_whole(e):
        return pltpu.make_async_remote_copy(
            src_ref=near_recv[e],
            dst_ref=near_recv[e],
            send_sem=near_send_sems.at[e],
            recv_sem=near_recv_sems.at[e],
            device_id=(around[0],),
            device_id_type=MESH,
        )

    def far_whole(e):
        return pltpu.make_async_remote_copy(
            src_ref=far_recv[e],
            dst_ref=far_recv[e],
            send_sem=far_send_sems.at[e],
            recv_sem=far_recv_sems.at[e],
            device_id=(around[0],),
            device_id_type=MESH,
        )

    def slot_of(held, other):
        pair = (min(held, other), max(held, other))
        return PAIRS.index(pair), (0 if held <= other else 1)

    def make_links(links, i):
        for t in range(3):
            places = edge_tile(X_LINK, i, t, False).astype(jnp.int32)
            for d in range(6):
                place = spread_row(places[d : d + 1])
                lower = None if d == 2 * t else slot_of(d, 2 * t + 1)[1]
                upper = None if d == 2 * t + 1 else slot_of(d, 2 * t)[1]
                low_at = jnp.zeros_like(place) if lower is None else LANES + 64 * lower + (place & 63)
                up_at = jnp.zeros_like(place) if upper is None else LANES + 64 * upper + (place & 63)
                links[t * 6 + d] = jnp.where(place >= LANES, jnp.where(first_half, low_at, up_at), 0)

    def finish_merge(e, totals, links, inverse, owned):
        near_whole(e).wait_recv()
        for i, total in enumerate(totals):
            back = [jnp.where(first_half, near_recv[e][2 * t + 1, i], near_recv[e][2 * t, i]) for t in range(3)]
            for k in range(owned):
                total[k] = total[k] + returned(inverse, back, k)
        far_whole(e).wait_recv()
        for i, total in enumerate(totals):
            for t in range(3):
                value = total[owned + t] + jnp.where(
                    first_half, near_recv[e][2 * t, i], near_recv[e][2 * t + 1, i]
                )
                for d in range(6):
                    at = links[t * 6 + d]
                    sources = []
                    if d != 2 * t:
                        sources.append(far_recv[e][slot_of(d, 2 * t + 1)[0], i])
                    if d != 2 * t + 1:
                        sources.append(far_recv[e][slot_of(d, 2 * t)[0], i])
                    found = [take(source, at & 127) for source in sources]
                    term = found[0] if len(found) == 1 else jnp.where(first_half, found[0], found[1])
                    value = value + jnp.where(at >= LANES, term, 0.0)
                total[owned + t] = value

    def reduce_start(slot, stage, tile):
        mine = (low, high)[stage]
        ar_send[slot] = tile
        ar_recv[slot, mine] = tile
        for partner in groups[stage]:
            pltpu.make_async_remote_copy(
                src_ref=ar_send.at[slot],
                dst_ref=ar_recv.at[slot, mine],
                send_sem=ar_send_sems.at[slot],
                recv_sem=ar_recv_sems.at[slot],
                device_id=(partner,),
                device_id_type=MESH,
            ).start()

    def reduce_whole(slot, stage):
        part = ar_recv.at[slot, pl.ds(0, (LOW, highs)[stage] - 1)]
        return pltpu.make_async_remote_copy(
            src_ref=part,
            dst_ref=part,
            send_sem=ar_send_sems.at[slot],
            recv_sem=ar_recv_sems.at[slot],
            device_id=(around[0],),
            device_id_type=MESH,
        )

    def reduce_finish(slot, stage):
        reduce_whole(slot, stage).wait_recv()
        parts = [ar_recv[slot, i] for i in range((LOW, highs)[stage])]
        while len(parts) > 1:
            parts = [a + b for a, b in zip(parts[::2], parts[1::2])]
        return parts[0]

    def gather(out, lanes, blocks, count, sources, first, last, unroll):
        def body(i, carry):
            r, c = lanes[i], blocks[i]
            for o, s in zip(out, sources):
                value = zero8 if first == 0 else o[i]
                for k in range(first, last):
                    value = jnp.where(c == k, take(s[k], r), value)
                o[i] = value
            return carry

        lax.fori_loop(0, count, body, 0, unroll=unroll)

    def pick(source, lanes, blocks, t, owned):
        value = zero8
        for k in range(owned):
            value = jnp.where(blocks[t] == k, take(source[k], lanes[t]), value)
        return value

    def returned(inverse, tiles, block):
        value = None
        for d in range(6):
            where = inverse[block * 6 + d]
            term = jnp.where(where >= LANES, take(tiles[d // 2], where & 127), 0.0)
            value = term if value is None else value + term
        return value

    def index_tables(row, lanes, blocks, i):
        lanes[i] = spread_row(row & 127)
        blocks[i] = spread_row(row >> 7)

    def masks(qm, blocks, count, parts):
        def body(i, carry):
            c = blocks[i]
            for q in range(parts):
                one = jnp.where(c == q, 1.0, 0.0)
                qm[pl.ds(16 * q, 16), cols(i * LANES)] = jnp.concatenate([one, one], 0).astype(bf16)
            return carry

        lax.fori_loop(0, count, body, 0, unroll=4)

    def one_hot(column):
        return jnp.where(jnp.broadcast_to(column, (LANES, LANES)) == lane128, 1.0, 0.0).astype(bf16)

    def columns_of(rows):
        count, width = rows.shape
        padded = -count % 8
        if padded:
            rows = jnp.concatenate([rows, jnp.zeros((padded, width), jnp.int32)], axis=0)
        return (rows & 127).astype(f32).T

    def fill(base, qm, first, last, count, source, unroll=10):
        def body(i, carry):
            term = st[pl.ds(source, 16), cols(i * LANES)]
            for q in range(first, last):
                left[pl.ds(base + 16 * (q - first), 16), cols(i * LANES)] = (
                    term * qm[pl.ds(16 * q, 16), cols(i * LANES)]
                )
            return carry

        lax.fori_loop(0, count, body, 0, unroll=unroll)

    def scatter(rows, width, table):
        return jnp.dot(left[0:rows, 0:width], table[...], preferred_element_type=f32)

    def joined(product, q):
        return product[16 * q : 16 * q + 8] + product[16 * q + 8 : 16 * q + 16]

    def apply(matrix, values, size, group, consume):
        def body(jj, carry):
            for h in range(2):
                total = [None] * group
                for k in range(size):
                    value = values[2 * k + h]
                    for u in range(group):
                        row = matrix[jj * group + u, pl.ds(k, 1), pl.ds(LANES * h, LANES)]
                        term = row * value
                        total[u] = term if k == 0 else total[u] + term
                for u in range(group):
                    carry = consume(2 * (jj * group + u) + h, total[u], carry)
            return carry

        return body

    def shared_rows(ref, width):
        rows = []
        for t in range(3):
            pieces = []
            for d in (2 * t, 2 * t + 1):
                pieces.append(ref[d : d + 1, :])
                if width < 64:
                    pieces.append(jnp.full((1, 64 - width), -LANES, jnp.int32))
            rows.append(jnp.concatenate(pieces, axis=1))
        return rows

    edge_rows = shared_rows(send_edge_ref, 64)
    for t in range(3):
        index_tables(edge_rows[t], sr, sc, t)
    for k in range(EB):
        xe[k] = x_ref[:, LANES * k : LANES * (k + 1)]
        pe[k] = p_ref[:, LANES * k : LANES * (k + 1)]
    for t in range(3):
        send_bufs[X_PAIR][t, 0] = pick(xe, sr, sc, t, EB)
        send_bufs[X_PAIR][t, 1] = pick(pe, sr, sc, t, EB)

    for j in range(EDOF):
        for h in range(2):
            row = elem_edge_ref[j : j + 1, LANES * h : LANES * (h + 1)]
            index_tables(row, er, ec, 2 * j + h)
    edge_columns = columns_of(elem_edge_ref[...])
    for j in range(EDOF):
        for h in range(2):
            oh_e[256 * j + LANES * h : 256 * j + LANES * (h + 1), :] = one_hot(
                edge_columns[LANES * h : LANES * (h + 1), j : j + 1]
            )
    masks(qm_e, ec, 2 * EDOF, EG)

    loads[0].wait()
    for j in range(EDOF):
        for h in range(2):
            diagonal = spread_row(stiff_ref[j, j : j + 1, LANES * h : LANES * (h + 1)])
            st[0:16, 256 * j + LANES * h : 256 * j + LANES * (h + 1)] = split(diagonal)
    fill(0, qm_e, 0, EG, 2 * EDOF, 0)
    product = scatter(16 * EG, ECOL, oh_e)
    for k in range(EG):
        recip[k] = joined(product, k)

    def merge_start(e, totals, lanes, blocks, owned):
        ghosts = [[total[owned + t] for t in range(3)] for total in totals]
        far_start(e, ghosts)
        shares = [[pick(total, lanes, blocks, t, owned) for t in range(3)] for total in totals]
        near_start(e, shares, ghosts)


    def inverse_lists(inverse, rows, lanes, blocks, owned, i):
        turned = columns_of(jnp.concatenate(rows, axis=0))
        table = jnp.concatenate([one_hot(turned[:, t : t + 1]) for t in range(3)], axis=0)
        parts = []
        for q in range(0, owned + owned % 2):
            line = []
            for t in range(3):
                keep = jnp.logical_and(row8 == 2 * t + (lane8 >> 6), blocks[t] == q)
                line.append(jnp.where(keep, LANES + lane8, 0).astype(f32))
            parts.append(jnp.concatenate(line, axis=1))
        found = jnp.dot(
            jnp.concatenate(parts, axis=0).astype(bf16), table, preferred_element_type=f32
        )
        places = [found[8 * q : 8 * q + 8] for q in range(owned)]
        for t in range(3):
            send_bufs[X_LINK][t, i] = pick(places, lanes, blocks, t, owned)
        for q in range(owned):
            place = places[q].astype(jnp.int32)
            for d in range(6):
                inverse[q * 6 + d] = spread_row(place[d : d + 1])

    inverse_lists(inv_e, edge_rows, sr, sc, EB, 0)
    node_rows = shared_rows(send_node_ref, 32)
    for t in range(3):
        index_tables(node_rows[t], tr, tc, t)
    inverse_lists(inv_n, node_rows, tr, tc, NB, 1)
    pl.semaphore_wait(barrier, len(everyone))
    for t in range(3):
        launch(X_PAIR, t)
    for t in range(3):
        launch(X_LINK, t)
    merge_start(M_DIAG, [recip], sr, sc, EB)
    gather([vx], er, ec, 2 * EDOF, [xe], 0, EB, 20)

    arrived(X_PAIR)
    for t in range(3):
        xe[EB + t] = edge_tile(X_PAIR, 0, t, False)
        pe[EB + t] = edge_tile(X_PAIR, 1, t, False)
    gather([vx], er, ec, 2 * EDOF, [xe], EB, EG, 20)

    def keep_terms(base, store, ghost_base, i, total):
        term = split(total)
        place = cols(i * LANES)
        if store is not None:
            image_t[pl.ds(store, 16), place] = term
        if base is not None:
            st[pl.ds(base, 16), place] = term
            for q in range(EB, EG):
                left[pl.ds(ghost_base + 16 * (q - EB), 16), place] = term * qm_e[pl.ds(16 * q, 16), place]

    def x_consume(base, store, ghost_base):
        def consume(i, total, carry):
            keep_terms(base, store, ghost_base, i, total)
            return carry + total * vx[i]

        return consume

    loads[1].wait()
    numerator = lax.fori_loop(0, 5, apply(stiff_ref, vx, EDOF, 4, x_consume(0, 0, 0)), zero8, unroll=5)
    denominator = lax.fori_loop(0, 5, apply(mass_ref, vx, EDOF, 4, x_consume(16, 16, 48)), zero8, unroll=5)
    numerator = jnp.sum(numerator, axis=1, keepdims=True)
    denominator = jnp.sum(denominator, axis=1, keepdims=True)
    reduce_start(0, 0, jnp.where(lane8 == 0, numerator, jnp.where(lane8 == 1, denominator, 0.0)))
    product = scatter(96, ECOL, oh_e)
    ghosts = [[joined(product, 3 * i + t) for t in range(3)] for i in range(2)]
    far_start(M_IMAGE, ghosts)
    for t in range(3):
        tot[EB + t] = ghosts[0][t]
        tot2[EB + t] = ghosts[1][t]
    fill(0, qm_e, 0, EB, 2 * EDOF, 0)
    fill(16 * EB, qm_e, 0, EB, 2 * EDOF, 16)
    product = scatter(32 * EB, ECOL, oh_e)
    for k in range(EB):
        tot[k] = joined(product, k)
        tot2[k] = joined(product, EB + k)
    near_start(
        M_IMAGE,
        [[pick(total, sr, sc, t, EB) for t in range(3)] for total in (tot, tot2)],
        [[total[EB + t] for t in range(3)] for total in (tot, tot2)],
    )
    center = 0.5 * (interval_high + interval_low)
    spread = 0.5 * (interval_high - interval_low)
    arrived(X_LINK)
    make_links(link_e, 0)
    make_links(link_n, 1)
    reduce_start(1, 1, reduce_finish(0, 0))
    finish_merge(M_DIAG, [recip], link_e, inv_e, EB)
    for k in range(EG):
        recip[k] = 1.0 / recip[k]

    def padded(index):
        ghost = index - LANES * NB
        return jnp.where(ghost < 0, index, LANES * NB + ((ghost >> 5) << 6) + (ghost & 31))

    for j in range(NDOF):
        for h in range(2):
            row = padded(elem_node_ref[j : j + 1, LANES * h : LANES * (h + 1)])
            index_tables(row, nr, nc, 2 * j + h)
    node_columns = columns_of(padded(elem_node_ref[...]))
    for j in range(NDOF):
        for h in range(2):
            oh_n[256 * j + LANES * h : 256 * j + LANES * (h + 1), :] = one_hot(
                node_columns[LANES * h : LANES * (h + 1), j : j + 1]
            )
    masks(qm_n, nc, 2 * NDOF, NG)

    finish_merge(M_IMAGE, [tot, tot2], link_e, inv_e, EB)
    for k in range(EG):
        scaled = recip[k] * (1.0 / center)
        ve[k] = tot[k] * scaled
        step[k] = tot2[k] * scaled
    gather([vv, vp], er, ec, 2 * EDOF, [ve, step], 0, EG, 20)
    sums = reduce_finish(1, 1)
    quotient = jnp.broadcast_to(sums[:, 0:1] / sums[:, 1:2], (8, LANES))

    def combine(i, carry):
        vv[i] = vv[i] - quotient * vp[i]
        return carry

    lax.fori_loop(0, 2 * EDOF, combine, 0, unroll=8)
    for k in range(EG):
        residual = tot[k] - quotient * tot2[k]
        res[k] = residual
        first_step = residual * recip[k] * (1.0 / center)
        step[k] = first_step
        ve[k] = first_step

    def stiff_terms(gathered):
        if not gathered:
            gather([vv], er, ec, 2 * EDOF, [ve], 0, EG, 20)

        def consume(i, total, carry):
            keep_terms(0, None, 0, i, total)
            return carry

        lax.fori_loop(0, 5, apply(stiff_ref, vv, EDOF, 4, consume), 0, unroll=5)
        product = scatter(48, ECOL, oh_e)
        return [joined(product, t) for t in range(3)]

    def stiff_owned():
        fill(0, qm_e, 0, EB, 2 * EDOF, 0)
        product = scatter(16 * EB, ECOL, oh_e)
        for k in range(EB):
            tot[k] = joined(product, k)

    sigma = center / spread
    rho_now = 1.0 / sigma
    for turn in range(CHEB_DEG - 1):
        rho_next = 1.0 / (2.0 * sigma - rho_now)
        ghosts = stiff_terms(turn == 0)
        far_start(M_CHEB + turn, [ghosts])
        for t in range(3):
            tot[EB + t] = ghosts[t]
        stiff_owned()
        near_start(
            M_CHEB + turn,
            [[pick(tot, sr, sc, t, EB) for t in range(3)]],
            [[tot[EB + t] for t in range(3)]],
        )
        if turn == 0:
            loads[2].wait()
            for j in range(NDOF):
                for h in range(2):
                    diagonal = spread_row(nodal_ref[j, j : j + 1, LANES * h : LANES * (h + 1)])
                    st[0:16, 256 * j + LANES * h : 256 * j + LANES * (h + 1)] = split(diagonal)
            fill(0, qm_n, 0, NG, 2 * NDOF, 0)
            product = scatter(16 * NG, NCOL, oh_n)
            for k in range(NG):
                nrecip[k] = joined(product, k)
            merge_start(M_NDIAG, [nrecip], tr, tc, NB)
        else:
            for side in range(2):
                for k in range(EB):
                    row = padded(grad_ref[1 - side : 2 - side, LANES * k : LANES * (k + 1)])
                    index_tables(row, gr, gc, side * EB + k)
            grad_columns = columns_of(padded(grad_ref[...]))
            for side in range(2):
                for k in range(EB):
                    oh_g[LANES * (side * EB + k) : LANES * (side * EB + k + 1), :] = one_hot(
                        grad_columns[LANES * k : LANES * (k + 1), 1 - side : 2 - side]
                    )
            masks(qm_g, gc, 2 * EB, NG)
        finish_merge(M_CHEB + turn, [tot], link_e, inv_e, EB)
        for k in range(EG):
            remain = res[k] - tot[k]
            new_step = rho_next * rho_now * step[k] + (2.0 * rho_next / spread) * remain * recip[k]
            step[k] = new_step
            ve[k] = ve[k] + new_step
        rho_now = rho_next
    ghosts = stiff_terms(False)
    for t in range(3):
        send_bufs[X_RETURN][t, 0] = ghosts[t]
        launch(X_RETURN, t)
    stiff_owned()
    finish_merge(M_NDIAG, [nrecip], link_n, inv_n, NB)
    for k in range(NG):
        padding = jnp.logical_and(k >= NB, (lane8 & 63) >= 32)
        nrecip[k] = 1.0 / jnp.where(padding, 1.0, nrecip[k])
    arrived(X_RETURN)
    tiles = [edge_tile(X_RETURN, 0, t, True) for t in range(3)]
    for k in range(EB):
        after = split(res[k] - (tot[k] + returned(inv_e, tiles, k)))
        st[0:16, LANES * k : LANES * (k + 1)] = after
        st[0:16, LANES * (EB + k) : LANES * (EB + k + 1)] = -after

    def node_start(e, qm, width, table, blocks):
        fill(0, qm, 0, NG, blocks, 0)
        product = scatter(16 * NG, width, table)
        for k in range(NG):
            ntot[k] = joined(product, k)
        merge_start(e, [ntot], tr, tc, NB)

    node_start(M_NODE, qm_g, GCOL, oh_g, 2 * EB)

    gather([vp], er, ec, 2 * EDOF, [pe], 0, EG, 20)

    def p_consume(store):
        def consume(i, total, carry):
            keep_terms(None, store, 0, i, total)
            return carry

        return consume

    lax.fori_loop(0, 5, apply(stiff_ref, vp, EDOF, 4, p_consume(32)), 0, unroll=5)
    lax.fori_loop(0, 5, apply(mass_ref, vp, EDOF, 4, p_consume(48)), 0, unroll=5)
    finish_merge(M_NODE, [ntot], link_n, inv_n, NB)
    for k in range(NG):
        nres[k] = ntot[k]
        first = jacobi_weight * ntot[k] * nrecip[k]
        nfirst[k] = first
        ne[k] = first
    gather([nv], nr, nc, 2 * NDOF, [ne], 0, NG, 20)

    def node_consume(i, total, carry):
        st[pl.ds(0, 16), cols(i * LANES)] = split(total)
        return carry

    lax.fori_loop(0, 5, apply(nodal_ref, nv, NDOF, 2, node_consume), 0, unroll=5)
    node_start(M_NODE + 1, qm_n, NCOL, oh_n, 2 * NDOF)

    def keep_basis(values, base):
        def body(i, carry):
            basis_t[pl.ds(base, 16), cols(i * LANES)] = split(values[i])
            return carry

        lax.fori_loop(0, 2 * EDOF, body, 0, unroll=10)

    keep_basis(vx, 0)
    keep_basis(vp, 32)
    finish_merge(M_NODE + 1, [ntot], link_n, inv_n, NB)
    for k in range(NG):
        ne[k] = nfirst[k] + jacobi_weight * (nres[k] - ntot[k]) * nrecip[k]
    gather([gv], gr, gc, 2 * EB, [ne], 0, NG, 24)
    for k in range(EB):
        total = ve[k] + gv[k] - gv[EB + k]
        ve[k] = total
        w_ref[:, LANES * k : LANES * (k + 1)] = total

    for t in range(3):
        send_bufs[X_W][t, 0] = pick(ve, sr, sc, t, EB)
        launch(X_W, t)
    image_t[96:128, :] = jnp.zeros((32, ECOL), bf16)
    gather([vv], er, ec, 2 * EDOF, [ve], 0, EB, 20)
    arrived(X_W)
    for t in range(3):
        ve[EB + t] = edge_tile(X_W, 0, t, False)
    gather([vv], er, ec, 2 * EDOF, [ve], EB, EG, 20)
    lax.fori_loop(0, 5, apply(stiff_ref, vv, EDOF, 4, p_consume(64)), 0, unroll=5)
    lax.fori_loop(0, 5, apply(mass_ref, vv, EDOF, 4, p_consume(80)), 0, unroll=5)
    keep_basis(vv, 16)
    product = lax.dot_general(
        basis_t[...], image_t[...], (((1,), (1,)), ((), ())), preferred_element_type=f32
    )

    def basis_rows(b):
        rows = joined(product, b)
        return rows + pltpu.roll(rows, LANES - 8, 1)

    x_rows, w_rows, p_rows = basis_rows(0), basis_rows(1), basis_rows(2)
    even = lane8 % 16 < 8
    packed = jnp.where(
        lane8 < 96,
        jnp.where(even, w_rows, pltpu.roll(x_rows, 8, 1)),
        jnp.where(even, pltpu.roll(p_rows, 64, 1), pltpu.roll(p_rows, 40, 1)),
    )
    reduce_start(2, 0, packed)
    reduce_start(3, 1, reduce_finish(2, 0))
    full = reduce_finish(3, 1) * (1.0 / (devices * LANES * EB))
    turned = full.T
    for m, out in enumerate((gram_s_ref, gram_m_ref)):

        def piece(at):
            return full[:, at : at + 8]

        xs, ps, ws = 16 * m, 32 + 16 * m, 64 + 16 * m
        upper = jnp.concatenate([piece(xs + 8), piece(ws + 8), piece(ps + 8)], axis=1)
        middle = jnp.concatenate([piece(xs), piece(ws), piece(ps)], axis=1)
        lower = jnp.concatenate(
            [turned[ps + 8 : ps + 16, :], piece(104 + 16 * m), piece(96 + 16 * m)], axis=1
        )
        out[...] = jnp.concatenate([upper, middle, lower], axis=0)

    for e in range(len(PLAIN)):
        whole(e).wait_send()
    for e in range(len(MERGED)):
        near_whole(e).wait_send()
        far_whole(e).wait_send()
    for slot in range(4):
        reduce_whole(slot, slot % 2).wait_send()


def solution(mesh):
    devices = mesh.shape["dom"]

    def shards(*arrays):
        def tiles(*lead):
            return pltpu.VMEM((*lead, 8, LANES), f32)

        def integers(count):
            return pltpu.VMEM((count, 8, LANES), jnp.int32)

        def halves(rows, width):
            return pltpu.VMEM((rows, width), bf16)

        scratch = [
            pltpu.VMEM(arrays[2].shape, f32),
            pltpu.VMEM(arrays[3].shape, f32),
            pltpu.VMEM(arrays[4].shape, f32),
            tiles(EG),
            tiles(EG),
            tiles(EG),
            tiles(NG),
            tiles(2 * EDOF),
            tiles(2 * EDOF),
            tiles(2 * EDOF),
            tiles(2 * NDOF),
            tiles(2 * EB),
            integers(2 * EDOF),
            integers(2 * EDOF),
            integers(2 * NDOF),
            integers(2 * NDOF),
            integers(2 * EB),
            integers(2 * EB),
            integers(3),
            integers(3),
            integers(3),
            integers(3),
            integers(6 * EB),
            integers(6 * NB),
            integers(18),
            integers(18),
            halves(ECOL, LANES),
            halves(16 * EG, ECOL),
            halves(NCOL, LANES),
            halves(16 * NG, NCOL),
            halves(GCOL, LANES),
            halves(16 * NG, GCOL),
            halves(32, ECOL),
            halves(32 * EB, ECOL),
            halves(48, ECOL),
            halves(128, ECOL),
            tiles(EG),
            tiles(EG),
            tiles(EG),
            tiles(EG),
            tiles(EG),
            tiles(NG),
            tiles(NG),
            tiles(NG),
            tiles(NG),
            [tiles(3, count) for count in PLAIN],
            [tiles(6, count) for count in PLAIN],
            [tiles(6, count) for count in MERGED],
            [tiles(6, count) for count in MERGED],
            [tiles(len(PAIRS), count) for count in MERGED],
            [tiles(len(PAIRS), count) for count in MERGED],
            tiles(4),
            tiles(4, max(LOW, devices // LOW)),
            pltpu.SemaphoreType.DMA((3,)),
            pltpu.SemaphoreType.DMA((len(PLAIN),)),
            pltpu.SemaphoreType.DMA((len(PLAIN),)),
            pltpu.SemaphoreType.DMA((len(MERGED),)),
            pltpu.SemaphoreType.DMA((len(MERGED),)),
            pltpu.SemaphoreType.DMA((len(MERGED),)),
            pltpu.SemaphoreType.DMA((len(MERGED),)),
            pltpu.SemaphoreType.DMA((4,)),
            pltpu.SemaphoreType.DMA((4,)),
        ]
        vmem = pl.BlockSpec(memory_space=pltpu.VMEM)
        return pl.pallas_call(
            lambda *refs: kernel(devices, *refs),
            out_shape=(
                jax.ShapeDtypeStruct((8, LANES * EB), f32),
                jax.ShapeDtypeStruct((24, 24), f32),
                jax.ShapeDtypeStruct((24, 24), f32),
            ),
            in_specs=[vmem] * 2 + [pl.BlockSpec(memory_space=pl.ANY)] * 3 + [vmem] * 5,
            out_specs=(vmem, vmem, vmem),
            scratch_shapes=scratch,
            compiler_params=pltpu.CompilerParams(
                collective_id=0, has_side_effects=True, vmem_limit_bytes=56 * 1024 * 1024
            ),
        )(*arrays)

    split_last = P(None, "dom")
    matrices = P(None, None, "dom")
    in_specs = (split_last,) * 2 + (matrices,) * 3 + (split_last,) * 5
    out_specs = (split_last, P(), P())
    return jax.shard_map(shards, mesh=mesh, in_specs=in_specs, out_specs=out_specs, check_vma=False)
```
